32 devices in a mesh: ctx: 32 (over z, y, x, core), head: 1.
Axes of the slice: x: 2, y: 2, z: 4, core: 2. Of those that a mesh axis runs over, the one named last changes fastest.
Arguments:
- fw_q: bfloat16 [8192, 2048], P('ctx', 'head'), may hold values from -6 to 6
- fw_k: bfloat16 [8192, 2048], P('ctx', 'head'), may hold values from -16 to 16
- fw_v: bfloat16 [8192, 2048], P('ctx', 'head'), may hold values from -6 to 6
- fw_lr: float32 [8192, 4], P('ctx', 'head'), may hold values from 0.1 to 3
- fast_gate: bfloat16 [4, 512, 512], P('head'), may hold values from -0.25 to 0.25
- fast_up: bfloat16 [4, 512, 512], P('head'), may hold values from -0.25 to 0.25
- fast_down: bfloat16 [4, 512, 512], P('head'), may hold values from -0.25 to 0.25
- attn_q: bfloat16 [8192, 2048], P('ctx', 'head'), may hold values from -96 to 96
- attn_k: bfloat16 [8192, 2048], P('ctx', 'head'), may hold values from -10 to 10
- attn_v: bfloat16 [8192, 2048], P('ctx', 'head'), may hold values from -6 to 6
Outputs:
- mixed_out: bfloat16 [8192, 2048], P(('ctx', 'head'))
The draws below stay inside these ranges and needn't reach their ends.
All inputs are finite; a program needn't handle non-finite values.
Results may differ from the reference program's by a relative error of at most 0.0095.
Values may be sent and summed in bfloat16 or wider, within the bound.
A program may use at most 128 MiB of HBM per device.

```python
import math
import jax
import jax.numpy as jnp
from jax import lax

DH = 512
FW_HEADS = 4
SWA_DH = 128
WINDOW = 128
NS_ITERS = 2
D = 2048
SWA_HEADS = 16
TOKENS = 8192


def draw_fw_k(key, part):
    key_scale, key_base = jax.random.split(jax.random.fold_in(key, 11), 2)
    scales = jnp.exp(jax.random.uniform(key_scale, (D,), jnp.float32, 0.0, math.log(10.0)))
    scales = scales / jnp.sqrt(jnp.mean(scales * scales))
    base = jnp.clip(jax.random.normal(key_base, (TOKENS, D), jnp.float32), -6.0, 6.0)
    return (base * scales[None, :]).astype(jnp.bfloat16)


def draw_fw_lr(key, part):
    ramp = 1.0 + 2.0 * jnp.arange(TOKENS, dtype=jnp.float32)[:, None] / (TOKENS - 1)
    base = jnp.exp(jax.random.uniform(jax.random.fold_in(key, 13), (TOKENS, FW_HEADS), jnp.float32, math.log(0.1), 0.0))
    return base * ramp


def attention_pair(key):
    key_q, key_k = jax.random.split(jax.random.fold_in(key, 23), 2)
    queries = 1.5 * jnp.clip(jax.random.normal(key_q, (TOKENS, D), jnp.float32), -6.0, 6.0)
    key_rows = 1.5 * jnp.clip(jax.random.normal(key_k, (TOKENS, D), jnp.float32), -6.0, 6.0)
    return (queries, key_rows)


def draw_attn_q(key, part):
    return attention_pair(key)[0].astype(jnp.bfloat16)


def draw_attn_k(key, part):
    return attention_pair(key)[1].astype(jnp.bfloat16)


def block_levels(stream_key, shape, cuts, smallest, largest):
    level = 1.0
    for dim, parts in cuts:
        draws = jax.random.uniform(jax.random.fold_in(jax.random.fold_in(stream_key, 6), dim), (parts,), jnp.float32, smallest / len(cuts), largest / len(cuts))
        level = level * jnp.repeat(jnp.exp(draws), shape[dim] // parts).reshape((-1,) + (1,) * (len(shape) - 1 - dim))
    return level


def centred(rng, shape, width, bound, cuts=(), kind=jnp.bfloat16):
    entries = width * jax.random.normal(rng, shape, jnp.float32)
    if cuts:
        entries = entries * block_levels(rng, shape, cuts, -0.22, 0.18)
    return jnp.clip(entries, -bound, bound).astype(kind)


def setup_inputs(seed: int = 0) -> dict:
    key_list = jax.random.split(jax.random.key(seed), 11)
    fw_q = centred(key_list[0], (TOKENS, D), 1.0, 6.0, ((0, 32),))
    fw_k = draw_fw_k(jax.random.fold_in(key_list[10], 71), 0)
    fw_v = centred(key_list[2], (TOKENS, D), 1.0, 6.0, ((0, 32),))
    fw_lr = draw_fw_lr(jax.random.fold_in(key_list[10], 71), 0)
    fast_gate = centred(key_list[4], (FW_HEADS, DH, DH), DH ** -0.5, 0.25)
    fast_up = centred(key_list[5], (FW_HEADS, DH, DH), DH ** -0.5, 0.25)
    fast_down = centred(key_list[6], (FW_HEADS, DH, DH), DH ** -0.5, 0.25)
    attn_q = draw_attn_q(jax.random.fold_in(key_list[10], 71), 0)
    attn_k = draw_attn_k(jax.random.fold_in(key_list[10], 71), 0)
    attn_v = centred(key_list[9], (TOKENS, D), 1.0, 6.0, ((0, 32),))
    return {"fw_q": fw_q, "fw_k": fw_k, "fw_v": fw_v, "fw_lr": fw_lr, "fast_gate": fast_gate, "fast_up": fast_up, "fast_down": fast_down, "attn_q": attn_q, "attn_k": attn_k, "attn_v": attn_v}


linear_coef = 3.4445
square_coef = -4.775
quartic_coef = 2.0315
epsilon = 1e-06

def mat_prod(left, right):
    return jnp.dot(left, right, preferred_element_type=jnp.float32)

def head_gradients(key_rows, value_rows, rates, gate_weight, up_weight, down_weight):
    pre_gate = mat_prod(key_rows, gate_weight)
    pre_up = mat_prod(key_rows, up_weight)
    sigmoid_gate = jax.nn.sigmoid(pre_gate)
    activated = pre_gate * sigmoid_gate
    hidden = (activated * pre_up).astype(jnp.bfloat16)
    out_grad = (-(rates[:, None] * value_rows.astype(jnp.float32))).astype(jnp.bfloat16)
    grad_down = mat_prod(hidden.T, out_grad)
    hidden_grad = mat_prod(out_grad, down_weight.T)
    slope = sigmoid_gate * (1.0 + pre_gate * (1.0 - sigmoid_gate))
    gate_grad = (hidden_grad * pre_up * slope).astype(jnp.bfloat16)
    up_grad = (hidden_grad * activated).astype(jnp.bfloat16)
    grad_gate = mat_prod(key_rows.T, gate_grad)
    grad_up = mat_prod(key_rows.T, up_grad)
    return (grad_gate, grad_up, grad_down)

def orthogonalize(gradient):
    iterate = (gradient / jnp.sqrt(jnp.sum(gradient * gradient) + epsilon)).astype(jnp.bfloat16)
    for sweep_index in range(NS_ITERS):
        gram_matrix = mat_prod(iterate, iterate.T).astype(jnp.bfloat16)
        square = mat_prod(gram_matrix, gram_matrix)
        polynomial = (square_coef * gram_matrix.astype(jnp.float32) + quartic_coef * square).astype(jnp.bfloat16)
        iterate = (linear_coef * iterate.astype(jnp.float32) + mat_prod(polynomial, iterate)).astype(jnp.bfloat16)
    return iterate

def refresh(weight, update):
    initial = weight.astype(jnp.float32)
    stepped = initial - update.astype(jnp.float32)
    old_norm = jnp.sqrt(lax.optimization_barrier(jnp.sum(initial * initial, axis=-2, keepdims=True)) + epsilon)
    new_norm = jnp.sqrt(lax.optimization_barrier(jnp.sum(stepped * stepped, axis=-2, keepdims=True)) + epsilon)
    return (stepped * (old_norm / new_norm)).astype(jnp.bfloat16)

def answer(queries, gate_weight, up_weight, down_weight):
    pre_gate = mat_prod(queries, gate_weight)
    pre_up = mat_prod(queries, up_weight)
    query_hidden = (jax.nn.silu(pre_gate) * pre_up).astype(jnp.bfloat16)
    return mat_prod(query_hidden, down_weight)

def window_attention(queries, key_rows, value_rows):
    blocks = TOKENS // WINDOW
    padding = jnp.zeros((WINDOW, D), jnp.bfloat16)
    keys_padded = jnp.concatenate([padding, key_rows], axis=0)
    values_padded = jnp.concatenate([padding, value_rows], axis=0)
    score_scale = 1.0 / math.sqrt(SWA_DH)

    def one_block(block_index):
        offset = block_index * WINDOW
        query_blk = lax.dynamic_slice_in_dim(queries, offset, WINDOW, 0).astype(jnp.float32).reshape(WINDOW, SWA_HEADS, SWA_DH)
        key_blk = lax.dynamic_slice_in_dim(keys_padded, offset, 2 * WINDOW, 0).astype(jnp.float32).reshape(2 * WINDOW, SWA_HEADS, SWA_DH)
        value_blk = lax.dynamic_slice_in_dim(values_padded, offset, 2 * WINDOW, 0).astype(jnp.float32).reshape(2 * WINDOW, SWA_HEADS, SWA_DH)
        scores = jnp.einsum('qhd,khd->hqk', query_blk, key_blk) * score_scale
        query_pos = offset + jnp.arange(WINDOW, dtype=jnp.int32)
        key_pos = offset - WINDOW + jnp.arange(2 * WINDOW, dtype=jnp.int32)
        allowed = (key_pos[None, :] <= query_pos[:, None]) & (key_pos[None, :] > query_pos[:, None] - WINDOW) & (key_pos[None, :] >= 0)
        masked = jnp.where(allowed[None, :, :], scores, -jnp.inf)
        row_peak = lax.optimization_barrier(jnp.max(masked, axis=-1, keepdims=True))
        exponent = jnp.exp(masked - row_peak)
        row_total = lax.optimization_barrier(jnp.sum(exponent, axis=-1, keepdims=True))
        weights_bf = (exponent / row_total).astype(jnp.bfloat16)
        result = jnp.einsum('hqk,khd->qhd', weights_bf.astype(jnp.float32), value_blk)
        return result.reshape(WINDOW, D)
    return lax.map(one_block, jnp.arange(blocks, dtype=jnp.int32)).reshape(TOKENS, D)

def reference(fw_q, fw_k, fw_v, fw_lr, fast_gate, fast_up, fast_down, attn_q, attn_k, attn_v):
    pieces = []
    for head_index in range(FW_HEADS):
        offset = head_index * DH
        gradients = head_gradients(fw_k[:, offset:offset + DH], fw_v[:, offset:offset + DH], fw_lr[:, head_index], fast_gate[head_index], fast_up[head_index], fast_down[head_index])
        weights = (fast_gate[head_index], fast_up[head_index], fast_down[head_index])
        renewed = [refresh(weights[matrix_index], orthogonalize(gradients[matrix_index])) for matrix_index in range(3)]
        pieces.append(answer(fw_q[:, offset:offset + DH], renewed[0], renewed[1], renewed[2]).astype(jnp.bfloat16))
    memory = jnp.concatenate(pieces, axis=1)
    attended = window_attention(attn_q, attn_k, attn_v)
    return (memory.astype(jnp.float32) + attended).astype(jnp.bfloat16)
```

```python
import functools
import math

import jax
import jax.numpy as jnp
from jax import lax
from jax.experimental import pallas as pl
from jax.experimental.pallas import tpu as pltpu
from jax.sharding import PartitionSpec as P

SWA_DH = 128
WINDOW = 128
NS_ITERS = 2
PIECES = 4

linear_coef = 3.4445
square_coef = -4.775
quartic_coef = 2.0315
epsilon = 1e-06

BF16 = jnp.bfloat16
F32 = jnp.float32
MESH = pl.DeviceIdType.MESH


def mat(left, right):
    return jnp.dot(left, right, preferred_element_type=F32)


def mat_tb(left, right):
    return lax.dot_general(left, right, (((1,), (1,)), ((), ())), preferred_element_type=F32)


def mat_ta(left, right):
    return lax.dot_general(left, right, (((0,), (0,)), ((), ())), preferred_element_type=F32)


def sigmoid(value):
    return 1.0 / (1.0 + jnp.exp(-value))


def flip(index, turn, count):
    bit = 1
    while bit < count:
        turn_bit = lax.rem(lax.div(turn, bit), 2)
        index_bit = lax.rem(lax.div(index, bit), 2)
        index = index + turn_bit * (bit - 2 * bit * index_bit)
        bit *= 2
    return index


def kernel(sizes, *refs):
    ctx, heads, chain, rows, width, model, attn = sizes
    fw_q, fw_k, fw_v, fw_lr, w_gate, w_up, w_down = refs[:7]
    refs = refs[7:]
    if attn:
        attn_q, attn_k, attn_v = refs[:3]
        refs = refs[3:]
    out = refs[0]
    (keys, grads, queries, grad_out, answers, returned, values, rates, weights, renewed,
     total, core_out, core_in, chain_out, chain_in, iter_a, iter_b, gram, poly,
     local_sem, key_s, key_r, og_s, og_r, q_s, q_r, ans_s, ans_r,
     core_s, core_r, chain_s, chain_r, cast_s, cast_r, side_s, side_r) = refs[1:37]
    if attn:
        q_rows, key_window, value_window, attended, halo_s, halo_r = refs[37:]

    me = lax.axis_index("ctx")
    core = lax.rem(me, 2)
    head = lax.rem(lax.div(me, 2), heads)
    z = lax.div(me, 2 * heads)
    mate = me + 1 - 2 * core
    step = 2 * heads
    piece_rows = width // PIECES

    def partner(turn):
        return me + 2 * (flip(head, turn, heads) - head)

    def columns(index):
        return pl.ds(pl.multiple_of(index * width, 128), width)

    def remote(src, dst, send, recv, device):
        return pltpu.make_async_remote_copy(
            src_ref=src, dst_ref=dst, send_sem=send, recv_sem=recv,
            device_id={"ctx": device}, device_id_type=MESH,
        )

    local = [
        pltpu.make_async_copy(fw_v, values, local_sem.at[0]),
        pltpu.make_async_copy(fw_lr, rates, local_sem.at[1]),
        pltpu.make_async_copy(fw_k.at[:, columns(head)], keys.at[head], local_sem.at[2]),
        pltpu.make_async_copy(w_gate.at[head], weights.at[0], local_sem.at[3]),
        pltpu.make_async_copy(w_up.at[head], weights.at[1], local_sem.at[4]),
        pltpu.make_async_copy(w_down.at[head], weights.at[2], local_sem.at[5]),
        pltpu.make_async_copy(fw_q.at[:, columns(head)], queries.at[head], local_sem.at[6]),
    ]
    if attn:
        local += [
            pltpu.make_async_copy(attn_q, q_rows, local_sem.at[7]),
            pltpu.make_async_copy(attn_k, key_window.at[pl.ds(WINDOW, rows)], local_sem.at[8]),
            pltpu.make_async_copy(attn_v, value_window.at[pl.ds(WINDOW, rows)], local_sem.at[9]),
        ]
    for copy in local:
        copy.start()

    barrier = pltpu.get_barrier_semaphore()

    def greet(device):
        pl.semaphore_signal(barrier, inc=1, device_id={"ctx": device}, device_id_type=MESH)

    for turn in range(1, heads):
        greet(partner(turn))
    greet(mate)
    expected = jnp.int32(heads)
    checks = [(z > 0, me - step), (z < chain - 1, me + step)]
    if attn:
        checks += [(me > 0, me - 1), (me < ctx - 1, me + 1)]
    for there, device in checks:
        pl.when(there)(functools.partial(greet, device))
        expected = expected + there.astype(jnp.int32)
    pl.semaphore_wait(barrier, expected)

    def key_copy(turn):
        other = flip(head, turn, heads)
        return remote(fw_k.at[:, columns(other)], keys.at[head], key_s.at[turn], key_r.at[turn],
                      partner(turn))

    def og_copy(turn):
        other = flip(head, turn, heads)
        return remote(grad_out.at[other], grads.at[head], og_s.at[turn], og_r.at[turn],
                      partner(turn))

    def query_copy(turn):
        other = flip(head, turn, heads)
        return remote(fw_q.at[:, columns(other)], queries.at[head], q_s.at[turn], q_r.at[turn],
                      partner(turn))

    def answer_copy(turn):
        return remote(answers.at[turn], returned.at[head], ans_s.at[turn], ans_r.at[turn],
                      partner(turn))

    for turn in range(1, heads):
        key_copy(turn).start()
    local[0].wait()
    local[1].wait()
    for index in range(heads):
        cols = slice(index * width, (index + 1) * width)
        grad_out[index] = (-(rates[:, index : index + 1] * values[:, cols].astype(F32))).astype(BF16)
    for turn in range(1, heads):
        og_copy(turn).start()

    def accumulate(key_ref, og_ref, first):
        key_rows = key_ref[...]
        og = og_ref[...]
        pre_gate = mat(key_rows, weights[0])
        pre_up = mat(key_rows, weights[1])
        hidden_grad = mat_tb(og, weights[2])
        sig = sigmoid(pre_gate)
        activated = pre_gate * sig
        hidden = (activated * pre_up).astype(BF16)
        gate_grad = (hidden_grad * pre_up * (sig * (1.0 + pre_gate * (1.0 - sig)))).astype(BF16)
        up_grad = (hidden_grad * activated).astype(BF16)
        for index, (left, right) in enumerate(
            ((key_rows, gate_grad), (key_rows, up_grad), (hidden, og))
        ):
            if first:
                total[index] = mat_ta(left, right)
            else:
                total[index] += mat_ta(left, right)

    for index in range(2, 6):
        local[index].wait()
    accumulate(keys.at[head], grad_out.at[head], True)

    if attn:
        score_scale = 1.0 / math.sqrt(SWA_DH)
        swa_heads = model // SWA_DH
        row_id = lax.broadcasted_iota(jnp.int32, (WINDOW, 2 * WINDOW), 0)
        col_id = lax.broadcasted_iota(jnp.int32, (WINDOW, 2 * WINDOW), 1)

        def attend(block):
            allowed = (col_id > row_id) & (col_id <= row_id + WINDOW)
            if block == 0:
                allowed = allowed & (col_id >= jnp.where(me == 0, WINDOW, 0))
            here = slice(block * WINDOW, (block + 1) * WINDOW)
            there = slice(block * WINDOW, (block + 2) * WINDOW)

            def one(index, carry):
                cols = pl.ds(pl.multiple_of(index * SWA_DH, SWA_DH), SWA_DH)
                scores = mat_tb(q_rows[here, cols], key_window[there, cols]) * score_scale
                masked = jnp.where(allowed, scores, -jnp.inf)
                peak = jnp.max(masked, axis=-1, keepdims=True)
                exponent = jnp.exp(masked - peak)
                probs = (exponent / jnp.sum(exponent, axis=-1, keepdims=True)).astype(BF16)
                attended[here, cols] = mat(probs, value_window[there, cols])
                return carry

            lax.fori_loop(0, swa_heads, one, 0, unroll=4 if swa_heads % 4 == 0 else 1)

        for index in range(7, 10):
            local[index].wait()
        for block in range(1, rows // WINDOW):
            attend(block)

    def gather_turn(turn, carry):
        key_copy(turn).wait_recv()
        og_copy(turn).wait_recv()
        other = flip(head, turn, heads)
        accumulate(keys.at[other], grads.at[other], False)
        return carry

    lax.fori_loop(1, heads, gather_turn, 0)

    def home(matrix):
        return jnp.minimum(matrix, 1)

    def root(matrix):
        return jnp.where(matrix == 1, chain - 1, 0)

    def toward(matrix):
        return jnp.where(matrix == 1, 1, -1)

    def part(piece):
        return pl.ds(piece * piece_rows, piece_rows)

    def core_copy(matrix, piece):
        return remote(core_out.at[matrix, part(piece)], core_in.at[matrix, part(piece)],
                      core_s.at[matrix, piece], core_r.at[matrix, piece], mate)

    def chain_copy(matrix, piece):
        return remote(chain_out.at[matrix, part(piece)], chain_in.at[matrix, part(piece)],
                      chain_s.at[matrix, piece], chain_r.at[matrix, piece],
                      me + step * toward(matrix))

    def cast_copy(matrix, piece):
        return remote(renewed.at[matrix, part(piece)], renewed.at[matrix, part(piece)],
                      cast_s.at[matrix, piece], cast_r.at[matrix, piece],
                      me - step * toward(matrix))

    def side_copy(matrix, piece):
        return remote(renewed.at[matrix, part(piece)], renewed.at[matrix, part(piece)],
                      side_s.at[matrix, piece], side_r.at[matrix, piece], mate)

    def starts(matrix):
        return z == chain - 1 - root(matrix)

    def ends(matrix):
        return z == root(matrix)

    for piece in range(PIECES):
        for matrix in range(3):
            @pl.when(core != min(matrix, 1))
            def _():
                core_out[matrix, part(piece)] = total[matrix, part(piece)].astype(BF16)
                core_copy(matrix, piece).start()

    for turn in range(1, heads):
        query_copy(turn).start()

    if attn:
        def halo_copy(which):
            source = (attn_k, attn_v)[which]
            target = (key_window, value_window)[which]
            return remote(source.at[pl.ds(rows - WINDOW, WINDOW)], target.at[pl.ds(0, WINDOW)],
                          halo_s.at[which], halo_r.at[which], me + 1)

        @pl.when(me < ctx - 1)
        def _():
            halo_copy(0).start()
            halo_copy(1).start()

        @pl.when(me == 0)
        def _():
            key_window[0:WINDOW] = jnp.zeros((WINDOW, model), BF16)
            value_window[0:WINDOW] = jnp.zeros((WINDOW, model), BF16)

    def sum_piece(matrix, piece, has_input):
        core_copy(matrix, piece).wait_recv()
        summed = total[matrix, part(piece)] + core_in[matrix, part(piece)].astype(F32)
        if has_input:
            chain_copy(matrix, piece).wait_recv()
            summed = summed + chain_in[matrix, part(piece)].astype(F32)

        @pl.when(ends(matrix))
        def _():
            total[matrix, part(piece)] = summed

        @pl.when(jnp.logical_not(ends(matrix)))
        def _():
            chain_out[matrix, part(piece)] = summed.astype(BF16)
            chain_copy(matrix, piece).start()

    def start_chain(matrix, carry):
        @pl.when((core == home(matrix)) & starts(matrix))
        def _():
            for piece in range(PIECES):
                sum_piece(matrix, piece, False)
        return carry

    lax.fori_loop(0, 3, start_chain, 0)

    order = [(0, 0)]
    for piece in range(1, PIECES):
        order += [(0, piece), (1, piece - 1)]
    order += [(1, PIECES - 1)]

    def sum_rest(matrix, piece):
        @pl.when(jnp.logical_not(starts(matrix)))
        def _():
            sum_piece(matrix, piece, True)

    @pl.when(core == 0)
    def _():
        for piece in range(PIECES):
            sum_rest(0, piece)

    near_sum = jnp.where(2 * z < chain, 1, 2)

    @pl.when(core == 1)
    def _():
        for which, piece in order:
            sum_rest(near_sum if which == 0 else 3 - near_sum, piece)

    half = min(256, width)
    tiles = width // half

    def tile_loop(body):
        def run(index, carry):
            body(pl.ds(pl.multiple_of(index * half, half), half))
            return carry
        lax.fori_loop(0, tiles, run, 0)

    def renew(matrix):
        gradient = total[matrix]
        norm = jnp.sqrt(jnp.sum(gradient * gradient) + epsilon)
        iter_a[...] = (gradient / norm).astype(BF16)
        source, target = iter_a, iter_b
        for _ in range(NS_ITERS):
            def gram_rows(here, source=source):
                gram[here, :] = mat_tb(source[here, :], source[...]).astype(BF16)

            def poly_rows(here):
                mine = gram[here, :]
                square = mat(mine, gram[...])
                poly[here, :] = (square_coef * mine.astype(F32) + quartic_coef * square).astype(BF16)

            def next_rows(here, source=source, target=target):
                target[here, :] = (
                    linear_coef * source[here, :].astype(F32) + mat(poly[here, :], source[...])
                ).astype(BF16)

            tile_loop(gram_rows)
            tile_loop(poly_rows)
            tile_loop(next_rows)
            source, target = target, source
        initial = weights[matrix].astype(F32)
        stepped = initial - source[...].astype(F32)
        old_norm = jnp.sqrt(jnp.sum(initial * initial, axis=0, keepdims=True) + epsilon)
        new_norm = jnp.sqrt(jnp.sum(stepped * stepped, axis=0, keepdims=True) + epsilon)
        renewed[matrix] = (stepped * (old_norm / new_norm)).astype(BF16)

    def pass_on(matrix, piece):
        @pl.when(jnp.logical_not(starts(matrix)))
        def _():
            cast_copy(matrix, piece).start()

        side_copy(matrix, piece).start()

    def renew_here(matrix, carry):
        @pl.when((core == home(matrix)) & ends(matrix))
        def _():
            renew(matrix)
            for piece in range(PIECES):
                pass_on(matrix, piece)
        return carry

    lax.fori_loop(0, 3, renew_here, 0)

    if attn:
        @pl.when(me > 0)
        def _():
            halo_copy(0).wait_recv()
            halo_copy(1).wait_recv()
        attend(0)

    def forward(matrix, piece):
        @pl.when(jnp.logical_not(ends(matrix)))
        def _():
            cast_copy(matrix, piece).wait_recv()
            pass_on(matrix, piece)

    @pl.when(core == 0)
    def _():
        for piece in range(PIECES):
            forward(0, piece)

    @pl.when(core == 1)
    def _():
        for which, piece in order:
            forward(3 - near_sum if which == 0 else near_sum, piece)

    for matrix in range(3):
        @pl.when(core != min(matrix, 1))
        def _():
            for piece in range(PIECES):
                side_copy(matrix, piece).wait_recv()

    def answer(query_ref):
        query_rows = query_ref[...]
        pre_gate = mat(query_rows, renewed[0])
        pre_up = mat(query_rows, renewed[1])
        hidden = (pre_gate * sigmoid(pre_gate) * pre_up).astype(BF16)
        return mat(hidden, renewed[2]).astype(BF16)

    def answer_turn(turn, carry):
        query_copy(turn).wait_recv()
        answers[turn] = answer(queries.at[flip(head, turn, heads)])
        answer_copy(turn).start()
        return carry

    lax.fori_loop(1, heads, answer_turn, 0)
    local[6].wait()
    answers[0] = answer(queries.at[head])

    def finish(value, index):
        if attn:
            value = (value.astype(F32) + attended[:, columns(index)]).astype(BF16)
        out[:, columns(index)] = value

    finish(answers[0], head)
    for turn in range(1, heads):
        answer_copy(turn).wait_recv()
        other = flip(head, turn, heads)
        finish(returned[other], other)

    for turn in range(1, heads):
        key_copy(turn).wait_send()
        og_copy(turn).wait_send()
        query_copy(turn).wait_send()
        answer_copy(turn).wait_send()
    if attn:
        @pl.when(me < ctx - 1)
        def _():
            halo_copy(0).wait_send()
            halo_copy(1).wait_send()
    for matrix in range(3):
        @pl.when(core != min(matrix, 1))
        def _():
            for piece in range(PIECES):
                core_copy(matrix, piece).wait_send()

        @pl.when(core == min(matrix, 1))
        def _():
            for piece in range(PIECES):
                side_copy(matrix, piece).wait_send()

            @pl.when(jnp.logical_not(ends(matrix)))
            def _():
                for piece in range(PIECES):
                    chain_copy(matrix, piece).wait_send()

            @pl.when(jnp.logical_not(starts(matrix)))
            def _():
                for piece in range(PIECES):
                    cast_copy(matrix, piece).wait_send()


def memory_call(attn, *arrays):
    rows = arrays[0].shape[0]
    heads, width = arrays[4].shape[:2]
    ctx = lax.axis_size("ctx")
    chain = ctx // (2 * heads)
    model = arrays[0].shape[1]
    swa_model = arrays[-1].shape[1]
    square = (width, width)
    tokens = (heads, rows, width)
    dma = pltpu.SemaphoreType.DMA
    scratch = [pltpu.VMEM(tokens, BF16)] * 6
    scratch += [
        pltpu.VMEM((rows, model), BF16),
        pltpu.VMEM((rows, heads), F32),
        pltpu.VMEM((3,) + square, BF16),
        pltpu.VMEM((3,) + square, BF16),
        pltpu.VMEM((3,) + square, F32),
    ]
    scratch += [pltpu.VMEM((3,) + square, BF16)] * 4
    scratch += [pltpu.VMEM(square, BF16)] * 4
    scratch += [dma((10,))]
    scratch += [dma((heads,))] * 8
    scratch += [dma((3, PIECES))] * 8
    if attn:
        scratch += [
            pltpu.VMEM((rows, swa_model), BF16),
            pltpu.VMEM((rows + WINDOW, swa_model), BF16),
            pltpu.VMEM((rows + WINDOW, swa_model), BF16),
            pltpu.VMEM((rows, swa_model), F32),
            dma((2,)),
            dma((2,)),
        ]
    sizes = (ctx, heads, chain, rows, width, swa_model, attn)
    flops = 2 * rows * heads * width * width * 9 + 6 * NS_ITERS * width**3
    return pl.pallas_call(
        functools.partial(kernel, sizes),
        out_shape=jax.ShapeDtypeStruct((rows, model), BF16),
        in_specs=[pl.BlockSpec(memory_space=pl.ANY)] * len(arrays),
        out_specs=pl.BlockSpec(memory_space=pltpu.VMEM),
        scratch_shapes=scratch,
        cost_estimate=pl.CostEstimate(
            flops=flops, bytes_accessed=8 * rows * model * 2, transcendentals=rows * model
        ),
        compiler_params=pltpu.CompilerParams(
            collective_id=0, has_side_effects=True, vmem_limit_bytes=50 * 1024 * 1024
        ),
    )(*arrays)


def passed_along(value, axis, steps):
    count = lax.axis_size(axis)
    first, last = (max(0, -steps), min(count, count - steps))
    return lax.ppermute(value, axis, [(source, source + steps) for source in range(first, last)])


def attend(query_rows, key_window, value_window, device_index):
    row_count = query_rows.shape[0]
    key_count = key_window.shape[0]
    head_total = query_rows.shape[1] // SWA_DH
    query_heads = query_rows.reshape(row_count, head_total, SWA_DH)
    key_heads = key_window.reshape(key_count, head_total, SWA_DH)
    value_heads = value_window.reshape(key_count, head_total, SWA_DH)
    score_scale = 1.0 / math.sqrt(SWA_DH)
    scores = (
        jnp.einsum("qhd,khd->hqk", query_heads, key_heads, preferred_element_type=jnp.float32)
        * score_scale
    )
    query_pos = device_index * row_count + jnp.arange(row_count, dtype=jnp.int32)
    key_pos = device_index * row_count - WINDOW + jnp.arange(key_count, dtype=jnp.int32)
    allowed = (
        (key_pos[None, :] <= query_pos[:, None])
        & (key_pos[None, :] > query_pos[:, None] - WINDOW)
        & (key_pos[None, :] >= 0)
    )
    masked = jnp.where(allowed[None, :, :], scores, -jnp.inf)
    row_peak = jnp.max(masked, axis=-1, keepdims=True)
    exponent = jnp.exp(masked - row_peak)
    row_total = jnp.sum(exponent, axis=-1, keepdims=True)
    weights_bf = (exponent / row_total).astype(jnp.bfloat16)
    result = jnp.einsum("hqk,khd->qhd", weights_bf, value_heads, preferred_element_type=jnp.float32)
    return result.reshape(row_count, head_total * SWA_DH)


def shards(fw_q, fw_k, fw_v, fw_lr, fast_gate, fast_up, fast_down, attn_q, attn_k, attn_v):
    fast = (fw_q, fw_k, fw_v, fw_lr, fast_gate, fast_up, fast_down)
    groups = lax.axis_size("head")
    if groups == 1:
        return memory_call(True, *fast, attn_q, attn_k, attn_v)
    tokens_here = fw_k.shape[0]
    row_count = tokens_here // groups
    device_index = lax.axis_index("ctx") * groups + lax.axis_index("head")
    tail_pairs = passed_along(jnp.stack([attn_k[-WINDOW:], attn_v[-WINDOW:]]), "ctx", 1)
    extended = jnp.concatenate([tail_pairs, jnp.stack([attn_k, attn_v])], axis=1)
    windows = jnp.stack(
        [
            extended[:, group_index * row_count : group_index * row_count + WINDOW + row_count]
            for group_index in range(groups)
        ]
    )
    query_parts = attn_q.reshape(groups, 1, row_count, attn_q.shape[1])
    got_q, got_kv = (
        lax.all_to_all(query_parts, "head", split_axis=0, concat_axis=3, tiled=True),
        lax.all_to_all(windows, "head", split_axis=0, concat_axis=3, tiled=True),
    )
    memory = memory_call(False, *fast)
    memory_rows = lax.all_to_all(memory, "head", split_axis=0, concat_axis=1, tiled=True)
    attended = attend(got_q[0, 0], got_kv[0, 0], got_kv[0, 1], device_index)
    return (memory_rows.astype(jnp.float32) + attended).astype(jnp.bfloat16)


def solution(mesh):
    in_specs = (
        P("ctx", "head"),
        P("ctx", "head"),
        P("ctx", "head"),
        P("ctx", "head"),
        P("head", None, None),
        P("head", None, None),
        P("head", None, None),
        P("ctx", "head"),
        P("ctx", "head"),
        P("ctx", "head"),
    )
    out_specs = P(("ctx", "head"), None)
    return jax.shard_map(shards, mesh=mesh, in_specs=in_specs, out_specs=out_specs, check_vma=False)
```

```python
import functools
import math

import jax
import jax.numpy as jnp
from jax import lax
from jax.experimental import pallas as pl
from jax.experimental.pallas import tpu as pltpu
from jax.sharding import PartitionSpec as P

SWA_DH = 128
WINDOW = 128
NS_ITERS = 2
PIECES = 4

linear_coef = 3.4445
square_coef = -4.775
quartic_coef = 2.0315
epsilon = 1e-06

BF16 = jnp.bfloat16
F32 = jnp.float32
MESH = pl.DeviceIdType.MESH


def mat(left, right):
    return jnp.dot(left, right, preferred_element_type=F32)


def mat_tb(left, right):
    return lax.dot_general(left, right, (((1,), (1,)), ((), ())), preferred_element_type=F32)


def mat_ta(left, right):
    return lax.dot_general(left, right, (((0,), (0,)), ((), ())), preferred_element_type=F32)


def sigmoid(value):
    return 1.0 / (1.0 + jnp.exp(-value))


def flip(index, turn, count):
    bit = 1
    while bit < count:
        turn_bit = lax.rem(lax.div(turn, bit), 2)
        index_bit = lax.rem(lax.div(index, bit), 2)
        index = index + turn_bit * (bit - 2 * bit * index_bit)
        bit *= 2
    return index


def kernel(sizes, *refs):
    ctx, heads, chain, rows, width, model, attn = sizes
    fw_q, fw_k, fw_v, fw_lr, w_gate, w_up, w_down = refs[:7]
    refs = refs[7:]
    if attn:
        attn_q, attn_k, attn_v = refs[:3]
        refs = refs[3:]
    out = refs[0]
    (keys, grads, queries, grad_out, answers, returned, hiddens, values, rates, weights, renewed,
     total, core_out, core_in, chain_out, chain_in, iter_a, iter_b, gram, poly,
     local_sem, key_s, key_r, og_s, og_r, q_s, q_r, ans_s, ans_r,
     core_s, core_r, chain_s, chain_r, cast_s, cast_r, side_s, side_r) = refs[1:38]
    if attn:
        q_rows, key_window, value_window, attended, relay, halo_s, halo_r, relay_s, relay_r = refs[38:]

    me = lax.axis_index("ctx")
    core = lax.rem(me, 2)
    head = lax.rem(lax.div(me, 2), heads)
    z = lax.div(me, 2 * heads)
    mate = me + 1 - 2 * core
    step = 2 * heads
    piece_rows = width // PIECES
    first = lax.rem(me, step) == 0
    last = lax.rem(me, step) == step - 1
    halo_to = me + 1 - jnp.where(last, step, 0)
    halo_from = me - 1 + jnp.where(first, step, 0)
    halo_sends = jnp.logical_not(last) | (z > 0)
    halo_comes = jnp.logical_not(first) | (z > 0)
    relay_sends = last & (z < chain - 1)
    relay_comes = last & (z > 0)

    def partner(turn):
        return me + 2 * (flip(head, turn, heads) - head)

    def columns(index):
        return pl.ds(pl.multiple_of(index * width, 128), width)

    def remote(src, dst, send, recv, device):
        return pltpu.make_async_remote_copy(
            src_ref=src, dst_ref=dst, send_sem=send, recv_sem=recv,
            device_id={"ctx": device}, device_id_type=MESH,
        )

    local = [
        pltpu.make_async_copy(fw_v, values, local_sem.at[0]),
        pltpu.make_async_copy(fw_lr, rates, local_sem.at[1]),
        pltpu.make_async_copy(fw_k.at[:, columns(head)], keys.at[head], local_sem.at[2]),
        pltpu.make_async_copy(w_gate.at[head], weights.at[0], local_sem.at[3]),
        pltpu.make_async_copy(w_up.at[head], weights.at[1], local_sem.at[4]),
        pltpu.make_async_copy(w_down.at[head], weights.at[2], local_sem.at[5]),
        pltpu.make_async_copy(fw_q.at[:, columns(head)], queries.at[head], local_sem.at[6]),
    ]
    if attn:
        local += [
            pltpu.make_async_copy(attn_q, q_rows, local_sem.at[7]),
            pltpu.make_async_copy(attn_k, key_window.at[pl.ds(WINDOW, rows)], local_sem.at[8]),
            pltpu.make_async_copy(attn_v, value_window.at[pl.ds(WINDOW, rows)], local_sem.at[9]),
        ]
    for copy in local:
        copy.start()

    barrier = pltpu.get_barrier_semaphore()

    def greet(device):
        pl.semaphore_signal(barrier, inc=1, device_id={"ctx": device}, device_id_type=MESH)

    for turn in range(1, heads):
        greet(partner(turn))
    greet(mate)
    expected = jnp.int32(heads)
    checks = [(z > 0, me - step), (z < chain - 1, me + step)]
    if attn:
        checks += [(halo_comes, halo_from), (halo_sends, halo_to)]
    for there, device in checks:
        pl.when(there)(functools.partial(greet, device))
        expected = expected + there.astype(jnp.int32)
    pl.semaphore_wait(barrier, expected)

    def key_copy(turn):
        other = flip(head, turn, heads)
        return remote(fw_k.at[:, columns(other)], keys.at[head], key_s.at[turn], key_r.at[turn],
                      partner(turn))

    def og_copy(turn):
        other = flip(head, turn, heads)
        return remote(grad_out.at[other], grads.at[head], og_s.at[turn], og_r.at[turn],
                      partner(turn))

    def query_copy(turn):
        other = flip(head, turn, heads)
        return remote(fw_q.at[:, columns(other)], queries.at[head], q_s.at[turn], q_r.at[turn],
                      partner(turn))

    def half_columns(part_index):
        return pl.ds(part_index * (width // 2), width // 2)

    def answer_copy(turn, part_index):
        cols = half_columns(part_index)
        return remote(answers.at[turn, :, cols], returned.at[head, :, cols],
                      ans_s.at[turn, part_index], ans_r.at[turn, part_index], partner(turn))

    for turn in range(1, heads):
        key_copy(turn).start()
    if attn:
        def relay_copy(which):
            source = (attn_k, attn_v)[which]
            return remote(source.at[pl.ds(rows - WINDOW, WINDOW)], relay.at[which],
                          relay_s.at[which], relay_r.at[which], me + step)

        @pl.when(relay_sends)
        def _():
            relay_copy(0).start()
            relay_copy(1).start()

    local[0].wait()
    local[1].wait()
    rate_columns = jnp.transpose(rates[...])
    for index in range(heads):
        cols = slice(index * width, (index + 1) * width)
        grad_out[index] = (
            -(rate_columns[:, index : index + 1] * values[:, cols].astype(F32))
        ).astype(BF16)
    for turn in range(1, heads):
        og_copy(turn).start()

    def accumulate(key_ref, og_ref, first):
        key_rows = key_ref[...]
        og = og_ref[...]
        pre_gate = mat(key_rows, weights[0])
        pre_up = mat(key_rows, weights[1])
        hidden_grad = mat_tb(og, weights[2])
        sig = sigmoid(pre_gate)
        activated = pre_gate * sig
        hidden = (activated * pre_up).astype(BF16)
        gate_grad = (hidden_grad * pre_up * (sig * (1.0 + pre_gate * (1.0 - sig)))).astype(BF16)
        up_grad = (hidden_grad * activated).astype(BF16)
        for index, (left, right) in enumerate(
            ((key_rows, gate_grad), (key_rows, up_grad), (hidden, og))
        ):
            if first:
                total[index] = mat_ta(left, right)
            else:
                total[index] += mat_ta(left, right)

    for index in range(2, 6):
        local[index].wait()
    accumulate(keys.at[head], grad_out.at[head], True)

    if attn:
        score_scale = 1.0 / math.sqrt(SWA_DH)
        swa_heads = model // SWA_DH
        row_id = lax.broadcasted_iota(jnp.int32, (WINDOW, 2 * WINDOW), 0)
        col_id = lax.broadcasted_iota(jnp.int32, (WINDOW, 2 * WINDOW), 1)

        def attend(block):
            allowed = (col_id > row_id) & (col_id <= row_id + WINDOW)
            if block == 0:
                allowed = allowed & (col_id >= jnp.where(me == 0, WINDOW, 0))
            here = slice(block * WINDOW, (block + 1) * WINDOW)
            there = slice(block * WINDOW, (block + 2) * WINDOW)

            def one(index, carry):
                cols = pl.ds(pl.multiple_of(index * SWA_DH, SWA_DH), SWA_DH)
                scores = mat_tb(q_rows[here, cols], key_window[there, cols]) * score_scale
                masked = jnp.where(allowed, scores, -jnp.inf)
                peak = jnp.max(masked, axis=-1, keepdims=True)
                exponent = jnp.exp(masked - peak)
                probs = (exponent / jnp.sum(exponent, axis=-1, keepdims=True)).astype(BF16)
                attended[here, cols] = mat(probs, value_window[there, cols])
                return carry

            lax.fori_loop(0, swa_heads, one, 0, unroll=4 if swa_heads % 4 == 0 else 1)

        for index in range(7, 10):
            local[index].wait()
        for block in range(1, rows // WINDOW):
            attend(block)

    def gather_turn(turn, carry):
        key_copy(turn).wait_recv()
        og_copy(turn).wait_recv()
        other = flip(head, turn, heads)
        accumulate(keys.at[other], grads.at[other], False)
        return carry

    lax.fori_loop(1, heads, gather_turn, 0)

    def home(matrix):
        return lax.rem(matrix, 2)

    def root(matrix):
        return jnp.where(matrix == 1, chain - 1, 0)

    def toward(matrix):
        return jnp.where(matrix == 1, 1, -1)

    def part(piece):
        return pl.ds(piece * piece_rows, piece_rows)

    def core_copy(matrix, piece):
        return remote(core_out.at[matrix, part(piece)], core_in.at[matrix, part(piece)],
                      core_s.at[matrix, piece], core_r.at[matrix, piece], mate)

    def chain_copy(matrix, piece):
        return remote(chain_out.at[matrix, part(piece)], chain_in.at[matrix, part(piece)],
                      chain_s.at[matrix, piece], chain_r.at[matrix, piece],
                      me + step * toward(matrix))

    def piece_columns(piece):
        return pl.ds(piece * piece_rows, piece_rows)

    def cast_copy(matrix, piece):
        here = renewed.at[matrix, :, piece_columns(piece)]
        return remote(here, here, cast_s.at[matrix, piece], cast_r.at[matrix, piece],
                      me - step * toward(matrix))

    def side_copy(matrix, piece):
        here = renewed.at[matrix, :, piece_columns(piece)]
        return remote(here, here, side_s.at[matrix, piece], side_r.at[matrix, piece], mate)

    def starts(matrix):
        return z == chain - 1 - root(matrix)

    def ends(matrix):
        return z == root(matrix)

    for matrices in ((0, 1), (2,)):
        for piece in range(PIECES):
            for matrix in matrices:
                @pl.when(core != matrix % 2)
                def _():
                    core_out[matrix, part(piece)] = total[matrix, part(piece)].astype(BF16)
                    core_copy(matrix, piece).start()

    for turn in range(1, heads):
        query_copy(turn).start()

    if attn:
        def halo_copy(which, relayed):
            source = (attn_k, attn_v)[which].at[pl.ds(rows - WINDOW, WINDOW)]
            if relayed:
                source = relay.at[which]
            target = (key_window, value_window)[which]
            return remote(source, target.at[pl.ds(0, WINDOW)],
                          halo_s.at[which], halo_r.at[which], halo_to)

        @pl.when(jnp.logical_not(last))
        def _():
            halo_copy(0, False).start()
            halo_copy(1, False).start()

        @pl.when(relay_comes)
        def _():
            for which in range(2):
                relay_copy(which).wait_recv()
                halo_copy(which, True).start()

        @pl.when(me == 0)
        def _():
            key_window[0:WINDOW] = jnp.zeros((WINDOW, model), BF16)
            value_window[0:WINDOW] = jnp.zeros((WINDOW, model), BF16)

    half = min(256, width)
    tiles = width // half

    def tile_loop(body):
        def run(index, carry):
            body(pl.ds(pl.multiple_of(index * half, half), half))
            return carry
        lax.fori_loop(0, tiles, run, 0)

    def renew(matrix):
        gradient = total[matrix]
        norm = jnp.sqrt(jnp.sum(gradient * gradient) + epsilon)
        iter_a[...] = (gradient / norm).astype(BF16)
        source, target = iter_a, iter_b
        for _ in range(NS_ITERS):
            def gram_rows(here, source=source):
                gram[here, :] = mat_tb(source[here, :], source[...]).astype(BF16)

            def poly_rows(here):
                mine = gram[here, :]
                square = mat(mine, gram[...])
                poly[here, :] = (square_coef * mine.astype(F32) + quartic_coef * square).astype(BF16)

            def next_rows(here, source=source, target=target):
                target[here, :] = (
                    linear_coef * source[here, :].astype(F32) + mat(poly[here, :], source[...])
                ).astype(BF16)

            tile_loop(gram_rows)
            tile_loop(poly_rows)
            tile_loop(next_rows)
            source, target = target, source
        initial = weights[matrix].astype(F32)
        stepped = initial - source[...].astype(F32)
        old_norm = jnp.sqrt(jnp.sum(initial * initial, axis=0, keepdims=True) + epsilon)
        new_norm = jnp.sqrt(jnp.sum(stepped * stepped, axis=0, keepdims=True) + epsilon)
        renewed[matrix] = (stepped * (old_norm / new_norm)).astype(BF16)

    def pass_on(matrix, piece):
        @pl.when(jnp.logical_not(starts(matrix)))
        def _():
            cast_copy(matrix, piece).start()

        side_copy(matrix, piece).start()

    def sum_piece(matrix, piece, behind):
        here = part(piece)
        core_copy(matrix, piece).wait_recv()
        total[matrix, here] += core_in[matrix, here].astype(F32)

        @pl.when(jnp.logical_not(starts(matrix)))
        def _():
            chain_copy(matrix, piece).wait_recv()
            total[matrix, here] += chain_in[matrix, here].astype(F32)

        @pl.when(jnp.logical_not(ends(matrix)))
        def _():
            chain_out[matrix, here] = total[matrix, here].astype(BF16)

            @pl.when(behind)
            def _():
                chain_copy(0, piece).wait_send()

            chain_copy(matrix, piece).start()

    def sum_and_renew(turn, carry):
        matrix = jnp.where(core == 0, 2 * turn, 1)

        @pl.when((core == 0) | (turn == 0))
        def _():
            for piece in range(PIECES):
                sum_piece(matrix, piece, turn == 1)

            @pl.when(ends(matrix))
            def _():
                renew(matrix)
                for piece in range(PIECES):
                    pass_on(matrix, piece)
        return carry

    lax.fori_loop(0, 2, sum_and_renew, 0)

    def take(matrix, piece):
        @pl.when((core == matrix % 2) & jnp.logical_not(ends(matrix)))
        def _():
            cast_copy(matrix, piece).wait_recv()
            pass_on(matrix, piece)

        @pl.when(core != matrix % 2)
        def _():
            side_copy(matrix, piece).wait_recv()

    @pl.when(core == 0)
    def _():
        for matrix in (0, 1):
            for piece in range(PIECES):
                take(matrix, piece)

    @pl.when(core == 1)
    def _():
        for matrix in (1, 0):
            for piece in range(PIECES):
                take(matrix, piece)

    def hide(turn, carry):
        query_rows = queries[flip(head, turn, heads)]
        pre_gate = mat(query_rows, renewed[0])
        pre_up = mat(query_rows, renewed[1])
        hiddens[turn] = (pre_gate * sigmoid(pre_gate) * pre_up).astype(BF16)
        return carry

    def hide_turn(turn, carry):
        query_copy(turn).wait_recv()
        return hide(turn, carry)

    middle = (heads + 2) // 2
    lax.fori_loop(1, middle, hide_turn, 0)
    for piece in range(PIECES):
        take(2, piece)
        if piece == 0:
            lax.fori_loop(middle, heads, hide_turn, 0)
        if 2 * (piece + 1) % PIECES == 0:
            part_index = 2 * (piece + 1) // PIECES - 1

            def answer_turn(turn, carry):
                cols = half_columns(part_index)
                answers[turn, :, cols] = mat(hiddens[turn], renewed[2, :, cols]).astype(BF16)
                answer_copy(turn, part_index).start()
                return carry

            lax.fori_loop(1, heads, answer_turn, 0)
    local[6].wait()
    hide(0, 0)
    answers[0] = mat(hiddens[0], renewed[2]).astype(BF16)

    if attn:
        @pl.when(halo_comes)
        def _():
            halo_copy(0, False).wait_recv()
            halo_copy(1, False).wait_recv()
        attend(0)

    def finish(value, index):
        if attn:
            value = (value.astype(F32) + attended[:, columns(index)]).astype(BF16)
        out[:, columns(index)] = value

    finish(answers[0], head)
    for turn in range(1, heads):
        for part_index in range(2):
            answer_copy(turn, part_index).wait_recv()
        other = flip(head, turn, heads)
        finish(returned[other], other)

    for turn in range(1, heads):
        key_copy(turn).wait_send()
        og_copy(turn).wait_send()
        query_copy(turn).wait_send()
        for part_index in range(2):
            answer_copy(turn, part_index).wait_send()
    if attn:
        @pl.when(halo_sends)
        def _():
            halo_copy(0, False).wait_send()
            halo_copy(1, False).wait_send()

        @pl.when(relay_sends)
        def _():
            relay_copy(0).wait_send()
            relay_copy(1).wait_send()
    for matrix in range(3):
        @pl.when(core != matrix % 2)
        def _():
            for piece in range(PIECES):
                core_copy(matrix, piece).wait_send()

        @pl.when(core == matrix % 2)
        def _():
            for piece in range(PIECES):
                side_copy(matrix, piece).wait_send()

            if matrix > 0:
                @pl.when(jnp.logical_not(ends(matrix)))
                def _():
                    for piece in range(PIECES):
                        chain_copy(matrix, piece).wait_send()

            @pl.when(jnp.logical_not(starts(matrix)))
            def _():
                for piece in range(PIECES):
                    cast_copy(matrix, piece).wait_send()


def memory_call(attn, *arrays):
    arrays = arrays[:3] + (arrays[3].T,) + arrays[4:]
    rows = arrays[0].shape[0]
    heads, width = arrays[4].shape[:2]
    ctx = lax.axis_size("ctx")
    chain = ctx // (2 * heads)
    model = arrays[0].shape[1]
    swa_model = arrays[-1].shape[1]
    square = (width, width)
    tokens = (heads, rows, width)
    dma = pltpu.SemaphoreType.DMA
    scratch = [pltpu.VMEM(tokens, BF16)] * 7
    scratch += [
        pltpu.VMEM((rows, model), BF16),
        pltpu.VMEM((heads, rows), F32),
        pltpu.VMEM((3,) + square, BF16),
        pltpu.VMEM((3,) + square, BF16),
        pltpu.VMEM((3,) + square, F32),
    ]
    scratch += [pltpu.VMEM((3,) + square, BF16)] * 4
    scratch += [pltpu.VMEM(square, BF16)] * 4
    scratch += [dma((10,))]
    scratch += [dma((heads,))] * 6
    scratch += [dma((heads, 2))] * 2
    scratch += [dma((3, PIECES))] * 8
    if attn:
        scratch += [
            pltpu.VMEM((rows, swa_model), BF16),
            pltpu.VMEM((rows + WINDOW, swa_model), BF16),
            pltpu.VMEM((rows + WINDOW, swa_model), BF16),
            pltpu.VMEM((rows, swa_model), F32),
            pltpu.VMEM((2, WINDOW, swa_model), BF16),
        ]
        scratch += [dma((2,))] * 4
    sizes = (ctx, heads, chain, rows, width, swa_model, attn)
    flops = 2 * rows * heads * width * width * 9 + 6 * NS_ITERS * width**3
    return pl.pallas_call(
        functools.partial(kernel, sizes),
        out_shape=jax.ShapeDtypeStruct((rows, model), BF16),
        in_specs=[pl.BlockSpec(memory_space=pl.ANY)] * len(arrays),
        out_specs=pl.BlockSpec(memory_space=pltpu.VMEM),
        scratch_shapes=scratch,
        cost_estimate=pl.CostEstimate(
            flops=flops, bytes_accessed=8 * rows * model * 2, transcendentals=rows * model
        ),
        compiler_params=pltpu.CompilerParams(
            collective_id=0, has_side_effects=True, vmem_limit_bytes=60 * 1024 * 1024
        ),
    )(*arrays)


def passed_along(value, axis, steps):
    count = lax.axis_size(axis)
    first, last = (max(0, -steps), min(count, count - steps))
    return lax.ppermute(value, axis, [(source, source + steps) for source in range(first, last)])


def attend(query_rows, key_window, value_window, device_index):
    row_count = query_rows.shape[0]
    key_count = key_window.shape[0]
    head_total = query_rows.shape[1] // SWA_DH
    query_heads = query_rows.reshape(row_count, head_total, SWA_DH)
    key_heads = key_window.reshape(key_count, head_total, SWA_DH)
    value_heads = value_window.reshape(key_count, head_total, SWA_DH)
    score_scale = 1.0 / math.sqrt(SWA_DH)
    scores = (
        jnp.einsum("qhd,khd->hqk", query_heads, key_heads, preferred_element_type=jnp.float32)
        * score_scale
    )
    query_pos = device_index * row_count + jnp.arange(row_count, dtype=jnp.int32)
    key_pos = device_index * row_count - WINDOW + jnp.arange(key_count, dtype=jnp.int32)
    allowed = (
        (key_pos[None, :] <= query_pos[:, None])
        & (key_pos[None, :] > query_pos[:, None] - WINDOW)
        & (key_pos[None, :] >= 0)
    )
    masked = jnp.where(allowed[None, :, :], scores, -jnp.inf)
    row_peak = jnp.max(masked, axis=-1, keepdims=True)
    exponent = jnp.exp(masked - row_peak)
    row_total = jnp.sum(exponent, axis=-1, keepdims=True)
    weights_bf = (exponent / row_total).astype(jnp.bfloat16)
    result = jnp.einsum("hqk,khd->qhd", weights_bf, value_heads, preferred_element_type=jnp.float32)
    return result.reshape(row_count, head_total * SWA_DH)


def shards(fw_q, fw_k, fw_v, fw_lr, fast_gate, fast_up, fast_down, attn_q, attn_k, attn_v):
    fast = (fw_q, fw_k, fw_v, fw_lr, fast_gate, fast_up, fast_down)
    groups = lax.axis_size("head")
    if groups == 1:
        return memory_call(True, *fast, attn_q, attn_k, attn_v)
    tokens_here = fw_k.shape[0]
    row_count = tokens_here // groups
    device_index = lax.axis_index("ctx") * groups + lax.axis_index("head")
    tail_pairs = passed_along(jnp.stack([attn_k[-WINDOW:], attn_v[-WINDOW:]]), "ctx", 1)
    extended = jnp.concatenate([tail_pairs, jnp.stack([attn_k, attn_v])], axis=1)
    windows = jnp.stack(
        [
            extended[:, group_index * row_count : group_index * row_count + WINDOW + row_count]
            for group_index in range(groups)
        ]
    )
    query_parts = attn_q.reshape(groups, 1, row_count, attn_q.shape[1])
    got_q, got_kv = (
        lax.all_to_all(query_parts, "head", split_axis=0, concat_axis=3, tiled=True),
        lax.all_to_all(windows, "head", split_axis=0, concat_axis=3, tiled=True),
    )
    memory = memory_call(False, *fast)
    memory_rows = lax.all_to_all(memory, "head", split_axis=0, concat_axis=1, tiled=True)
    attended = attend(got_q[0, 0], got_kv[0, 0], got_kv[0, 1], device_index)
    return (memory_rows.astype(jnp.float32) + attended).astype(jnp.bfloat16)


def solution(mesh):
    in_specs = (
        P("ctx", "head"),
        P("ctx", "head"),
        P("ctx", "head"),
        P("ctx", "head"),
        P("head", None, None),
        P("head", None, None),
        P("head", None, None),
        P("ctx", "head"),
        P("ctx", "head"),
        P("ctx", "head"),
    )
    out_specs = P(("ctx", "head"), None)
    return jax.shard_map(shards, mesh=mesh, in_specs=in_specs, out_specs=out_specs, check_vma=False)
```

```python
import functools
import math

import jax
import jax.numpy as jnp
from jax import lax
from jax.experimental import pallas as pl
from jax.experimental.pallas import tpu as pltpu
from jax.sharding import PartitionSpec as P

SWA_DH = 128
WINDOW = 128
NS_ITERS = 2
PIECES = 8

linear_coef = 3.4445
square_coef = -4.775
quartic_coef = 2.0315
epsilon = 1e-06

BF16 = jnp.bfloat16
F32 = jnp.float32
MESH = pl.DeviceIdType.MESH


def mat(left, right):
    return jnp.dot(left, right, preferred_element_type=F32)


def mat_tb(left, right):
    return lax.dot_general(left, right, (((1,), (1,)), ((), ())), preferred_element_type=F32)


def mat_ta(left, right):
    return lax.dot_general(left, right, (((0,), (0,)), ((), ())), preferred_element_type=F32)


def sigmoid(value):
    return 1.0 / (1.0 + jnp.exp(-value))


def flip(index, turn, count):
    bit = 1
    while bit < count:
        turn_bit = lax.rem(lax.div(turn, bit), 2)
        index_bit = lax.rem(lax.div(index, bit), 2)
        index = index + turn_bit * (bit - 2 * bit * index_bit)
        bit *= 2
    return index


def kernel(sizes, *refs):
    ctx, heads, chain, rows, width, model, attn = sizes
    fw_q, fw_k, fw_v, fw_lr, w_gate, w_up, w_down = refs[:7]
    refs = refs[7:]
    if attn:
        attn_q, attn_k, attn_v = refs[:3]
        refs = refs[3:]
    out = refs[0]
    (keys, grads, queries, grad_out, answers, returned, hiddens, values, rates, weights, renewed,
     total, core_out, core_in, chain_out, chain_in, iter_a, iter_b, gram, poly,
     local_sem, key_s, key_r, og_s, og_r, q_s, q_r, ans_s, ans_r,
     core_s, core_r, chain_s, chain_r, cast_s, cast_r, side_s, side_r) = refs[1:38]
    if attn:
        q_rows, key_window, value_window, attended, relay, halo_s, halo_r, relay_s, relay_r = refs[38:]

    me = lax.axis_index("ctx")
    core = lax.rem(me, 2)
    head = lax.rem(lax.div(me, 2), heads)
    z = lax.div(me, 2 * heads)
    mate = me + 1 - 2 * core
    step = 2 * heads
    piece_rows = width // PIECES
    first = lax.rem(me, step) == 0
    last = lax.rem(me, step) == step - 1
    halo_to = me + 1 - jnp.where(last, step, 0)
    halo_from = me - 1 + jnp.where(first, step, 0)
    halo_sends = jnp.logical_not(last) | (z > 0)
    halo_comes = jnp.logical_not(first) | (z > 0)
    relay_sends = last & (z < chain - 1)
    relay_comes = last & (z > 0)

    def partner(turn):
        return me + 2 * (flip(head, turn, heads) - head)

    def columns(index):
        return pl.ds(pl.multiple_of(index * width, 128), width)

    def remote(src, dst, send, recv, device):
        return pltpu.make_async_remote_copy(
            src_ref=src, dst_ref=dst, send_sem=send, recv_sem=recv,
            device_id={"ctx": device}, device_id_type=MESH,
        )

    local = [
        pltpu.make_async_copy(fw_v, values, local_sem.at[0]),
        pltpu.make_async_copy(fw_lr, rates, local_sem.at[1]),
        pltpu.make_async_copy(fw_k.at[:, columns(head)], keys.at[head], local_sem.at[2]),
        pltpu.make_async_copy(w_gate.at[head], weights.at[0], local_sem.at[3]),
        pltpu.make_async_copy(w_up.at[head], weights.at[1], local_sem.at[4]),
        pltpu.make_async_copy(w_down.at[head], weights.at[2], local_sem.at[5]),
        pltpu.make_async_copy(fw_q.at[:, columns(head)], queries.at[head], local_sem.at[6]),
    ]
    if attn:
        local += [
            pltpu.make_async_copy(attn_q, q_rows, local_sem.at[7]),
            pltpu.make_async_copy(attn_k, key_window.at[pl.ds(WINDOW, rows)], local_sem.at[8]),
            pltpu.make_async_copy(attn_v, value_window.at[pl.ds(WINDOW, rows)], local_sem.at[9]),
        ]
    for copy in local:
        copy.start()

    barrier = pltpu.get_barrier_semaphore()

    def greet(device):
        pl.semaphore_signal(barrier, inc=1, device_id={"ctx": device}, device_id_type=MESH)

    for turn in range(1, heads):
        greet(partner(turn))
    greet(mate)
    expected = jnp.int32(heads)
    checks = [(z > 0, me - step), (z < chain - 1, me + step)]
    if attn:
        checks += [(halo_comes, halo_from), (halo_sends, halo_to)]
    for there, device in checks:
        pl.when(there)(functools.partial(greet, device))
        expected = expected + there.astype(jnp.int32)
    pl.semaphore_wait(barrier, expected)

    def key_copy(turn):
        other = flip(head, turn, heads)
        return remote(fw_k.at[:, columns(other)], keys.at[head], key_s.at[turn], key_r.at[turn],
                      partner(turn))

    def og_copy(turn):
        other = flip(head, turn, heads)
        return remote(grad_out.at[other], grads.at[head], og_s.at[turn], og_r.at[turn],
                      partner(turn))

    def query_copy(turn):
        other = flip(head, turn, heads)
        return remote(fw_q.at[:, columns(other)], queries.at[head], q_s.at[turn], q_r.at[turn],
                      partner(turn))

    def half_columns(part_index):
        return pl.ds(part_index * (width // 2), width // 2)

    def answer_copy(turn, part_index):
        cols = half_columns(part_index)
        return remote(answers.at[turn, :, cols], returned.at[head, :, cols],
                      ans_s.at[turn, part_index], ans_r.at[turn, part_index], partner(turn))

    for turn in range(1, heads):
        key_copy(turn).start()
    if attn:
        def relay_copy(which):
            source = (attn_k, attn_v)[which]
            return remote(source.at[pl.ds(rows - WINDOW, WINDOW)], relay.at[which],
                          relay_s.at[which], relay_r.at[which], me + step)

        @pl.when(relay_sends)
        def _():
            relay_copy(0).start()
            relay_copy(1).start()

    local[0].wait()
    local[1].wait()
    rate_columns = jnp.transpose(rates[...])
    for index in range(heads):
        cols = slice(index * width, (index + 1) * width)
        grad_out[index] = (
            -(rate_columns[:, index : index + 1] * values[:, cols].astype(F32))
        ).astype(BF16)
    for turn in range(1, heads):
        og_copy(turn).start()

    def accumulate(key_ref, og_ref, first, done=None):
        key_rows = key_ref[...]
        og = og_ref[...]
        pre_gate = mat(key_rows, weights[0])
        pre_up = mat(key_rows, weights[1])
        hidden_grad = mat_tb(og, weights[2])
        sig = sigmoid(pre_gate)
        activated = pre_gate * sig
        gate_grad = (hidden_grad * pre_up * (sig * (1.0 + pre_gate * (1.0 - sig)))).astype(BF16)
        up_grad = (hidden_grad * activated).astype(BF16)
        hidden = (activated * pre_up).astype(BF16)
        for index, (left, right) in enumerate(
            ((key_rows, gate_grad), (key_rows, up_grad), (hidden, og))
        ):
            if first:
                total[index] = mat_ta(left, right)
            else:
                total[index] += mat_ta(left, right)
            if done is not None:
                done(index)

    for index in range(2, 6):
        local[index].wait()
    accumulate(keys.at[head], grad_out.at[head], True)

    if attn:
        score_scale = 1.0 / math.sqrt(SWA_DH)
        swa_heads = model // SWA_DH
        row_id = lax.broadcasted_iota(jnp.int32, (WINDOW, 2 * WINDOW), 0)
        col_id = lax.broadcasted_iota(jnp.int32, (WINDOW, 2 * WINDOW), 1)

        def attend(block):
            allowed = (col_id > row_id) & (col_id <= row_id + WINDOW)
            if block == 0:
                allowed = allowed & (col_id >= jnp.where(me == 0, WINDOW, 0))
            here = slice(block * WINDOW, (block + 1) * WINDOW)
            there = slice(block * WINDOW, (block + 2) * WINDOW)

            def one(index, carry):
                cols = pl.ds(pl.multiple_of(index * SWA_DH, SWA_DH), SWA_DH)
                scores = mat_tb(q_rows[here, cols], key_window[there, cols]) * score_scale
                masked = jnp.where(allowed, scores, -jnp.inf)
                peak = jnp.max(masked, axis=-1, keepdims=True)
                exponent = jnp.exp(masked - peak)
                probs = (exponent / jnp.sum(exponent, axis=-1, keepdims=True)).astype(BF16)
                attended[here, cols] = mat(probs, value_window[there, cols])
                return carry

            lax.fori_loop(0, swa_heads, one, 0, unroll=4 if swa_heads % 4 == 0 else 1)

        for index in range(7, 10):
            local[index].wait()
        for block in range(1, rows // WINDOW):
            attend(block)

    def root(matrix):
        return jnp.where(matrix == 1, chain - 1, 0)

    def toward(matrix):
        return jnp.where(matrix == 1, 1, -1)

    def part(piece):
        return pl.ds(piece * piece_rows, piece_rows)

    def core_copy(matrix, piece):
        return remote(core_out.at[matrix, part(piece)], core_in.at[matrix, part(piece)],
                      core_s.at[matrix, piece], core_r.at[matrix, piece], mate)

    def chain_copy(matrix, piece):
        return remote(chain_out.at[matrix, part(piece)], chain_in.at[matrix, part(piece)],
                      chain_s.at[matrix, piece], chain_r.at[matrix, piece],
                      me + step * toward(matrix))

    def block(matrix, piece):
        half = width // 2
        cols = 2 * width // PIECES
        return renewed.at[matrix, pl.ds(piece % 2 * half, half), pl.ds(piece // 2 * cols, cols)]

    def cast_copy(matrix, piece):
        here = block(matrix, piece)
        return remote(here, here, cast_s.at[matrix, piece], cast_r.at[matrix, piece],
                      me - step * toward(matrix))

    def side_copy(matrix, piece):
        here = block(matrix, piece)
        return remote(here, here, side_s.at[matrix, piece], side_r.at[matrix, piece], mate)

    def starts(matrix):
        return z == chain - 1 - root(matrix)

    def ends(matrix):
        return z == root(matrix)

    def exchange(matrix):
        @pl.when(core != matrix % 2)
        def _():
            for piece in range(PIECES):
                core_out[matrix, part(piece)] = total[matrix, part(piece)].astype(BF16)
                core_copy(matrix, piece).start()

    def gather_turn(turn, carry, done=None):
        key_copy(turn).wait_recv()
        og_copy(turn).wait_recv()
        other = flip(head, turn, heads)
        accumulate(keys.at[other], grads.at[other], False, done)
        return carry

    if heads > 1:
        lax.fori_loop(1, heads - 1, gather_turn, 0)
        gather_turn(heads - 1, 0, exchange)
    else:
        for matrix in range(3):
            exchange(matrix)

    for turn in range(1, heads):
        query_copy(turn).start()

    if attn:
        def halo_copy(which, relayed):
            source = (attn_k, attn_v)[which].at[pl.ds(rows - WINDOW, WINDOW)]
            if relayed:
                source = relay.at[which]
            target = (key_window, value_window)[which]
            return remote(source, target.at[pl.ds(0, WINDOW)],
                          halo_s.at[which], halo_r.at[which], halo_to)

        @pl.when(jnp.logical_not(last))
        def _():
            halo_copy(0, False).start()
            halo_copy(1, False).start()

        @pl.when(relay_comes)
        def _():
            for which in range(2):
                relay_copy(which).wait_recv()
                halo_copy(which, True).start()

        @pl.when(me == 0)
        def _():
            key_window[0:WINDOW] = jnp.zeros((WINDOW, model), BF16)
            value_window[0:WINDOW] = jnp.zeros((WINDOW, model), BF16)

    def renew(matrix):
        gradient = total[matrix]
        norm = jnp.sqrt(jnp.sum(gradient * gradient) + epsilon)
        iter_a[...] = (gradient * (1.0 / norm)).astype(BF16)
        source, target = iter_a, iter_b
        for _ in range(NS_ITERS):
            gram[...] = mat_tb(source[...], source[...]).astype(BF16)
            square = mat(gram[...], gram[...])
            poly[...] = (square_coef * gram[...].astype(F32) + quartic_coef * square).astype(BF16)
            target[...] = (
                linear_coef * source[...].astype(F32) + mat(poly[...], source[...])
            ).astype(BF16)
            source, target = target, source
        initial = weights[matrix].astype(F32)
        stepped = initial - source[...].astype(F32)
        old_norm = jnp.sqrt(jnp.sum(initial * initial, axis=0, keepdims=True) + epsilon)
        new_norm = jnp.sqrt(jnp.sum(stepped * stepped, axis=0, keepdims=True) + epsilon)
        renewed[matrix] = (stepped * (old_norm / new_norm)).astype(BF16)

    def pass_on(matrix, piece):
        @pl.when(jnp.logical_not(starts(matrix)))
        def _():
            cast_copy(matrix, piece).start()

        side_copy(matrix, piece).start()

    def sum_piece(matrix, piece, behind):
        here = part(piece)
        core_copy(matrix, piece).wait_recv()
        total[matrix, here] += core_in[matrix, here].astype(F32)

        @pl.when(jnp.logical_not(starts(matrix)))
        def _():
            chain_copy(matrix, piece).wait_recv()
            total[matrix, here] += chain_in[matrix, here].astype(F32)

        @pl.when(jnp.logical_not(ends(matrix)))
        def _():
            chain_out[matrix, here] = total[matrix, here].astype(BF16)

            @pl.when(behind)
            def _():
                chain_copy(0, piece).wait_send()

            chain_copy(matrix, piece).start()

    def sum_and_renew(turn, carry):
        matrix = jnp.where(core == 0, 2 * turn, 1)

        @pl.when((core == 0) | (turn == 0))
        def _():
            for piece in range(PIECES):
                sum_piece(matrix, piece, turn == 1)

            @pl.when(ends(matrix))
            def _():
                renew(matrix)
                for piece in range(PIECES):
                    pass_on(matrix, piece)
        return carry

    lax.fori_loop(0, 2, sum_and_renew, 0)

    def take(matrix, piece):
        @pl.when((core == matrix % 2) & jnp.logical_not(ends(matrix)))
        def _():
            cast_copy(matrix, piece).wait_recv()
            pass_on(matrix, piece)

        @pl.when(core != matrix % 2)
        def _():
            side_copy(matrix, piece).wait_recv()

    @pl.when(core == 0)
    def _():
        for matrix in (0, 1):
            for piece in range(PIECES):
                take(matrix, piece)

    @pl.when(core == 1)
    def _():
        for matrix in (1, 0):
            for piece in range(PIECES):
                take(matrix, piece)

    def hide(turn, carry):
        query_rows = queries[flip(head, turn, heads)]
        pre_gate = mat(query_rows, renewed[0])
        pre_up = mat(query_rows, renewed[1])
        hiddens[turn] = (pre_gate * sigmoid(pre_gate) * pre_up).astype(BF16)
        return carry

    def hide_turn(turn, carry):
        query_copy(turn).wait_recv()
        return hide(turn, carry)

    middle = (heads + 2) // 2
    lax.fori_loop(1, middle, hide_turn, 0)
    for piece in range(PIECES):
        take(2, piece)
        if piece == 0:
            lax.fori_loop(middle, heads, hide_turn, 0)
        if 2 * (piece + 1) % PIECES == 0:
            part_index = 2 * (piece + 1) // PIECES - 1

            def answer_turn(turn, carry):
                cols = half_columns(part_index)
                answers[turn, :, cols] = mat(hiddens[turn], renewed[2, :, cols]).astype(BF16)
                answer_copy(turn, part_index).start()
                return carry

            lax.fori_loop(1, heads, answer_turn, 0)
    local[6].wait()
    hide(0, 0)
    answers[0] = mat(hiddens[0], renewed[2]).astype(BF16)

    if attn:
        @pl.when(halo_comes)
        def _():
            halo_copy(0, False).wait_recv()
            halo_copy(1, False).wait_recv()
        attend(0)

    def finish(value, index):
        if attn:
            value = (value.astype(F32) + attended[:, columns(index)]).astype(BF16)
        out[:, columns(index)] = value

    finish(answers[0], head)
    for turn in range(1, heads):
        for part_index in range(2):
            answer_copy(turn, part_index).wait_recv()
        other = flip(head, turn, heads)
        finish(returned[other], other)

    for turn in range(1, heads):
        key_copy(turn).wait_send()
        og_copy(turn).wait_send()
        query_copy(turn).wait_send()
        for part_index in range(2):
            answer_copy(turn, part_index).wait_send()
    if attn:
        @pl.when(halo_sends)
        def _():
            halo_copy(0, False).wait_send()
            halo_copy(1, False).wait_send()

        @pl.when(relay_sends)
        def _():
            relay_copy(0).wait_send()
            relay_copy(1).wait_send()
    for matrix in range(3):
        @pl.when(core != matrix % 2)
        def _():
            for piece in range(PIECES):
                core_copy(matrix, piece).wait_send()

        @pl.when(core == matrix % 2)
        def _():
            for piece in range(PIECES):
                side_copy(matrix, piece).wait_send()

            if matrix > 0:
                @pl.when(jnp.logical_not(ends(matrix)))
                def _():
                    for piece in range(PIECES):
                        chain_copy(matrix, piece).wait_send()

            @pl.when(jnp.logical_not(starts(matrix)))
            def _():
                for piece in range(PIECES):
                    cast_copy(matrix, piece).wait_send()


def memory_call(attn, *arrays):
    arrays = arrays[:3] + (arrays[3].T,) + arrays[4:]
    rows = arrays[0].shape[0]
    heads, width = arrays[4].shape[:2]
    ctx = lax.axis_size("ctx")
    chain = ctx // (2 * heads)
    model = arrays[0].shape[1]
    swa_model = arrays[-1].shape[1]
    square = (width, width)
    tokens = (heads, rows, width)
    dma = pltpu.SemaphoreType.DMA
    scratch = [pltpu.VMEM(tokens, BF16)] * 7
    scratch += [
        pltpu.VMEM((rows, model), BF16),
        pltpu.VMEM((heads, rows), F32),
        pltpu.VMEM((3,) + square, BF16),
        pltpu.VMEM((3,) + square, BF16),
        pltpu.VMEM((3,) + square, F32),
    ]
    scratch += [pltpu.VMEM((3,) + square, BF16)] * 4
    scratch += [pltpu.VMEM(square, BF16)] * 4
    scratch += [dma((10,))]
    scratch += [dma((heads,))] * 6
    scratch += [dma((heads, 2))] * 2
    scratch += [dma((3, PIECES))] * 8
    if attn:
        scratch += [
            pltpu.VMEM((rows, swa_model), BF16),
            pltpu.VMEM((rows + WINDOW, swa_model), BF16),
            pltpu.VMEM((rows + WINDOW, swa_model), BF16),
            pltpu.VMEM((rows, swa_model), F32),
            pltpu.VMEM((2, WINDOW, swa_model), BF16),
        ]
        scratch += [dma((2,))] * 4
    sizes = (ctx, heads, chain, rows, width, swa_model, attn)
    flops = 2 * rows * heads * width * width * 9 + 6 * NS_ITERS * width**3
    return pl.pallas_call(
        functools.partial(kernel, sizes),
        out_shape=jax.ShapeDtypeStruct((rows, model), BF16),
        in_specs=[pl.BlockSpec(memory_space=pl.ANY)] * len(arrays),
        out_specs=pl.BlockSpec(memory_space=pltpu.VMEM),
        scratch_shapes=scratch,
        cost_estimate=pl.CostEstimate(
            flops=flops, bytes_accessed=8 * rows * model * 2, transcendentals=rows * model
        ),
        compiler_params=pltpu.CompilerParams(
            collective_id=0, has_side_effects=True, vmem_limit_bytes=60 * 1024 * 1024
        ),
    )(*arrays)


def passed_along(value, axis, steps):
    count = lax.axis_size(axis)
    first, last = (max(0, -steps), min(count, count - steps))
    return lax.ppermute(value, axis, [(source, source + steps) for source in range(first, last)])


def attend(query_rows, key_window, value_window, device_index):
    row_count = query_rows.shape[0]
    key_count = key_window.shape[0]
    head_total = query_rows.shape[1] // SWA_DH
    query_heads = query_rows.reshape(row_count, head_total, SWA_DH)
    key_heads = key_window.reshape(key_count, head_total, SWA_DH)
    value_heads = value_window.reshape(key_count, head_total, SWA_DH)
    score_scale = 1.0 / math.sqrt(SWA_DH)
    scores = (
        jnp.einsum("qhd,khd->hqk", query_heads, key_heads, preferred_element_type=jnp.float32)
        * score_scale
    )
    query_pos = device_index * row_count + jnp.arange(row_count, dtype=jnp.int32)
    key_pos = device_index * row_count - WINDOW + jnp.arange(key_count, dtype=jnp.int32)
    allowed = (
        (key_pos[None, :] <= query_pos[:, None])
        & (key_pos[None, :] > query_pos[:, None] - WINDOW)
        & (key_pos[None, :] >= 0)
    )
    masked = jnp.where(allowed[None, :, :], scores, -jnp.inf)
    row_peak = jnp.max(masked, axis=-1, keepdims=True)
    exponent = jnp.exp(masked - row_peak)
    row_total = jnp.sum(exponent, axis=-1, keepdims=True)
    weights_bf = (exponent / row_total).astype(jnp.bfloat16)
    result = jnp.einsum("hqk,khd->qhd", weights_bf, value_heads, preferred_element_type=jnp.float32)
    return result.reshape(row_count, head_total * SWA_DH)


def shards(fw_q, fw_k, fw_v, fw_lr, fast_gate, fast_up, fast_down, attn_q, attn_k, attn_v):
    fast = (fw_q, fw_k, fw_v, fw_lr, fast_gate, fast_up, fast_down)
    groups = lax.axis_size("head")
    if groups == 1:
        return memory_call(True, *fast, attn_q, attn_k, attn_v)
    tokens_here = fw_k.shape[0]
    row_count = tokens_here // groups
    device_index = lax.axis_index("ctx") * groups + lax.axis_index("head")
    tail_pairs = passed_along(jnp.stack([attn_k[-WINDOW:], attn_v[-WINDOW:]]), "ctx", 1)
    extended = jnp.concatenate([tail_pairs, jnp.stack([attn_k, attn_v])], axis=1)
    windows = jnp.stack(
        [
            extended[:, group_index * row_count : group_index * row_count + WINDOW + row_count]
            for group_index in range(groups)
        ]
    )
    query_parts = attn_q.reshape(groups, 1, row_count, attn_q.shape[1])
    got_q, got_kv = (
        lax.all_to_all(query_parts, "head", split_axis=0, concat_axis=3, tiled=True),
        lax.all_to_all(windows, "head", split_axis=0, concat_axis=3, tiled=True),
    )
    memory = memory_call(False, *fast)
    memory_rows = lax.all_to_all(memory, "head", split_axis=0, concat_axis=1, tiled=True)
    attended = attend(got_q[0, 0], got_kv[0, 0], got_kv[0, 1], device_index)
    return (memory_rows.astype(jnp.float32) + attended).astype(jnp.bfloat16)


def solution(mesh):
    in_specs = (
        P("ctx", "head"),
        P("ctx", "head"),
        P("ctx", "head"),
        P("ctx", "head"),
        P("head", None, None),
        P("head", None, None),
        P("head", None, None),
        P("ctx", "head"),
        P("ctx", "head"),
        P("ctx", "head"),
    )
    out_specs = P(("ctx", "head"), None)
    return jax.shard_map(shards, mesh=mesh, in_specs=in_specs, out_specs=out_specs, check_vma=False)
```

```python
import functools
import math

import jax
import jax.numpy as jnp
from jax import lax
from jax.experimental import pallas as pl
from jax.experimental.pallas import tpu as pltpu
from jax.sharding import PartitionSpec as P

SWA_DH = 128
WINDOW = 128
NS_ITERS = 2
PIECES = 8

linear_coef = 3.4445
square_coef = -4.775
quartic_coef = 2.0315
epsilon = 1e-06

BF16 = jnp.bfloat16
F32 = jnp.float32
MESH = pl.DeviceIdType.MESH


def mat(left, right):
    return jnp.dot(left, right, preferred_element_type=F32)


def mat_tb(left, right):
    return lax.dot_general(left, right, (((1,), (1,)), ((), ())), preferred_element_type=F32)


def mat_ta(left, right):
    return lax.dot_general(left, right, (((0,), (0,)), ((), ())), preferred_element_type=F32)


def sigmoid(value):
    return 1.0 / (1.0 + jnp.exp(-value))


def flip(index, turn, count):
    bit = 1
    while bit < count:
        turn_bit = lax.rem(lax.div(turn, bit), 2)
        index_bit = lax.rem(lax.div(index, bit), 2)
        index = index + turn_bit * (bit - 2 * bit * index_bit)
        bit *= 2
    return index


def kernel(sizes, *refs):
    ctx, heads, chain, rows, width, model, attn = sizes
    fw_q, fw_k, fw_v, fw_lr, w_gate, w_up, w_down = refs[:7]
    refs = refs[7:]
    if attn:
        attn_q, attn_k, attn_v = refs[:3]
        refs = refs[3:]
    out = refs[0]
    (keys, grads, queries, grad_out, answers, returned, hiddens, values, rates, weights, renewed,
     total, core_out, core_in, chain_out, chain_in, iter_a, iter_b, gram, poly,
     local_sem, key_s, key_r, og_s, og_r, q_s, q_r, ans_s, ans_r,
     core_s, core_r, chain_s, chain_r, cast_s, cast_r, side_s, side_r) = refs[1:38]
    if attn:
        q_rows, key_window, value_window, attended, relay, halo_s, halo_r, relay_s, relay_r = refs[38:]

    me = lax.axis_index("ctx")
    core = lax.rem(me, 2)
    head = lax.rem(lax.div(me, 2), heads)
    z = lax.div(me, 2 * heads)
    mate = me + 1 - 2 * core
    step = 2 * heads
    piece_rows = width // PIECES
    first = lax.rem(me, step) == 0
    last = lax.rem(me, step) == step - 1
    halo_to = me + 1 - jnp.where(last, step, 0)
    halo_from = me - 1 + jnp.where(first, step, 0)
    halo_sends = jnp.logical_not(last) | (z > 0)
    halo_comes = jnp.logical_not(first) | (z > 0)
    relay_sends = last & (z < chain - 1)
    relay_comes = last & (z > 0)

    def partner(turn):
        return me + 2 * (flip(head, turn, heads) - head)

    def columns(index):
        return pl.ds(pl.multiple_of(index * width, 128), width)

    def remote(src, dst, send, recv, device):
        return pltpu.make_async_remote_copy(
            src_ref=src, dst_ref=dst, send_sem=send, recv_sem=recv,
            device_id={"ctx": device}, device_id_type=MESH,
        )

    local = [
        pltpu.make_async_copy(fw_v, values, local_sem.at[0]),
        pltpu.make_async_copy(fw_lr, rates, local_sem.at[1]),
        pltpu.make_async_copy(fw_k.at[:, columns(head)], keys.at[head], local_sem.at[2]),
        pltpu.make_async_copy(w_gate.at[head], weights.at[0], local_sem.at[3]),
        pltpu.make_async_copy(w_up.at[head], weights.at[1], local_sem.at[4]),
        pltpu.make_async_copy(w_down.at[head], weights.at[2], local_sem.at[5]),
        pltpu.make_async_copy(fw_q.at[:, columns(head)], queries.at[head], local_sem.at[6]),
    ]
    if attn:
        local += [
            pltpu.make_async_copy(attn_q, q_rows, local_sem.at[7]),
            pltpu.make_async_copy(attn_k, key_window.at[pl.ds(WINDOW, rows)], local_sem.at[8]),
            pltpu.make_async_copy(attn_v, value_window.at[pl.ds(WINDOW, rows)], local_sem.at[9]),
        ]
    for copy in local:
        copy.start()

    barrier = pltpu.get_barrier_semaphore()

    def greet(device):
        pl.semaphore_signal(barrier, inc=1, device_id={"ctx": device}, device_id_type=MESH)

    for turn in range(1, heads):
        greet(partner(turn))
    greet(mate)
    expected = jnp.int32(heads)
    checks = [(z > 0, me - step), (z < chain - 1, me + step)]
    if attn:
        checks += [(halo_comes, halo_from), (halo_sends, halo_to)]
    for there, device in checks:
        pl.when(there)(functools.partial(greet, device))
        expected = expected + there.astype(jnp.int32)
    pl.semaphore_wait(barrier, expected)

    def key_copy(turn):
        other = flip(head, turn, heads)
        return remote(fw_k.at[:, columns(other)], keys.at[head], key_s.at[turn], key_r.at[turn],
                      partner(turn))

    def og_copy(turn):
        other = flip(head, turn, heads)
        return remote(grad_out.at[other], grads.at[head], og_s.at[turn], og_r.at[turn],
                      partner(turn))

    def query_copy(turn):
        other = flip(head, turn, heads)
        return remote(fw_q.at[:, columns(other)], queries.at[head], q_s.at[turn], q_r.at[turn],
                      partner(turn))

    def half_columns(part_index):
        return pl.ds(part_index * (width // 2), width // 2)

    def answer_copy(turn, part_index):
        cols = half_columns(part_index)
        return remote(answers.at[turn, :, cols], returned.at[head, :, cols],
                      ans_s.at[turn, part_index], ans_r.at[turn, part_index], partner(turn))

    for turn in range(1, heads):
        key_copy(turn).start()
    if attn:
        def relay_copy(which):
            source = (attn_k, attn_v)[which]
            return remote(source.at[pl.ds(rows - WINDOW, WINDOW)], relay.at[which],
                          relay_s.at[which], relay_r.at[which], me + step)

        @pl.when(relay_sends)
        def _():
            relay_copy(0).start()
            relay_copy(1).start()

    local[0].wait()
    local[1].wait()
    rate_columns = jnp.transpose(rates[...])
    for index in range(heads):
        cols = slice(index * width, (index + 1) * width)
        grad_out[index] = (
            -(rate_columns[:, index : index + 1] * values[:, cols].astype(F32))
        ).astype(BF16)
    for turn in range(1, heads):
        og_copy(turn).start()

    def accumulate(key_ref, og_ref, first, done=None):
        key_rows = key_ref[...]
        og = og_ref[...]
        pre_gate = mat(key_rows, weights[0])
        pre_up = mat(key_rows, weights[1])
        hidden_grad = mat_tb(og, weights[2])
        sig = sigmoid(pre_gate)
        activated = pre_gate * sig
        gate_grad = (hidden_grad * pre_up * (sig * (1.0 + pre_gate * (1.0 - sig)))).astype(BF16)
        up_grad = (hidden_grad * activated).astype(BF16)
        hidden = (activated * pre_up).astype(BF16)
        for index, (left, right) in enumerate(
            ((key_rows, gate_grad), (key_rows, up_grad), (hidden, og))
        ):
            if first:
                total[index] = mat_ta(left, right)
            else:
                total[index] += mat_ta(left, right)
            if done is not None:
                done(index)

    for index in range(2, 6):
        local[index].wait()
    accumulate(keys.at[head], grad_out.at[head], True)

    if attn:
        score_scale = 1.0 / math.sqrt(SWA_DH)
        swa_heads = model // SWA_DH
        row_id = lax.broadcasted_iota(jnp.int32, (WINDOW, 2 * WINDOW), 0)
        col_id = lax.broadcasted_iota(jnp.int32, (WINDOW, 2 * WINDOW), 1)

        def attend(block):
            allowed = (col_id > row_id) & (col_id <= row_id + WINDOW)
            if block == 0:
                allowed = allowed & (col_id >= jnp.where(me == 0, WINDOW, 0))
            here = slice(block * WINDOW, (block + 1) * WINDOW)
            there = slice(block * WINDOW, (block + 2) * WINDOW)

            def one(index, carry):
                cols = pl.ds(pl.multiple_of(index * SWA_DH, SWA_DH), SWA_DH)
                scores = mat_tb(q_rows[here, cols], key_window[there, cols]) * score_scale
                masked = jnp.where(allowed, scores, -jnp.inf)
                peak = jnp.max(masked, axis=-1, keepdims=True)
                exponent = jnp.exp(masked - peak)
                probs = (exponent / jnp.sum(exponent, axis=-1, keepdims=True)).astype(BF16)
                attended[here, cols] = mat(probs, value_window[there, cols])
                return carry

            lax.fori_loop(0, swa_heads, one, 0, unroll=4 if swa_heads % 4 == 0 else 1)

        for index in range(7, 10):
            local[index].wait()
        for block in range(1, rows // WINDOW):
            attend(block)

    def root(matrix):
        return jnp.where(matrix == 1, chain - 1, 0)

    def toward(matrix):
        return jnp.where(matrix == 1, 1, -1)

    def part(piece):
        return pl.ds(piece * piece_rows, piece_rows)

    def core_copy(matrix, piece):
        return remote(core_out.at[matrix, part(piece)], core_in.at[matrix, part(piece)],
                      core_s.at[matrix, piece], core_r.at[matrix, piece], mate)

    def chain_copy(matrix, piece):
        return remote(chain_out.at[matrix, part(piece)], chain_in.at[matrix, part(piece)],
                      chain_s.at[matrix, piece], chain_r.at[matrix, piece],
                      me + step * toward(matrix))

    def block(matrix, piece):
        half = width // 2
        cols = 2 * width // PIECES
        return renewed.at[matrix, pl.ds(piece % 2 * half, half), pl.ds(piece // 2 * cols, cols)]

    def cast_copy(matrix, piece):
        here = block(matrix, piece)
        return remote(here, here, cast_s.at[matrix, piece], cast_r.at[matrix, piece],
                      me - step * toward(matrix))

    def side_copy(matrix, piece):
        here = block(matrix, piece)
        return remote(here, here, side_s.at[matrix, piece], side_r.at[matrix, piece], mate)

    def starts(matrix):
        return z == chain - 1 - root(matrix)

    def ends(matrix):
        return z == root(matrix)

    def exchange(matrix):
        @pl.when(core != matrix % 2)
        def _():
            for piece in range(PIECES):
                core_out[matrix, part(piece)] = total[matrix, part(piece)].astype(BF16)
                core_copy(matrix, piece).start()

    def gather_turn(turn, carry, done=None):
        key_copy(turn).wait_recv()
        og_copy(turn).wait_recv()
        other = flip(head, turn, heads)
        accumulate(keys.at[other], grads.at[other], False, done)
        return carry

    if heads > 1:
        lax.fori_loop(1, heads - 1, gather_turn, 0)
        gather_turn(heads - 1, 0, exchange)
    else:
        for matrix in range(3):
            exchange(matrix)

    for turn in range(1, heads):
        query_copy(turn).start()

    if attn:
        def halo_copy(which, relayed):
            source = (attn_k, attn_v)[which].at[pl.ds(rows - WINDOW, WINDOW)]
            if relayed:
                source = relay.at[which]
            target = (key_window, value_window)[which]
            return remote(source, target.at[pl.ds(0, WINDOW)],
                          halo_s.at[which], halo_r.at[which], halo_to)

        @pl.when(jnp.logical_not(last))
        def _():
            halo_copy(0, False).start()
            halo_copy(1, False).start()

        @pl.when(relay_comes)
        def _():
            for which in range(2):
                relay_copy(which).wait_recv()
                halo_copy(which, True).start()

        @pl.when(me == 0)
        def _():
            key_window[0:WINDOW] = jnp.zeros((WINDOW, model), BF16)
            value_window[0:WINDOW] = jnp.zeros((WINDOW, model), BF16)

    def renew(matrix):
        gradient = total[matrix]
        norm = jnp.sqrt(jnp.sum(gradient * gradient) + epsilon)
        iter_a[...] = (gradient * (1.0 / norm)).astype(BF16)
        source, target = iter_a, iter_b
        for _ in range(NS_ITERS):
            gram[...] = mat_tb(source[...], source[...]).astype(BF16)
            square = mat(gram[...], gram[...])
            poly[...] = (square_coef * gram[...].astype(F32) + quartic_coef * square).astype(BF16)
            target[...] = (
                linear_coef * source[...].astype(F32) + mat(poly[...], source[...])
            ).astype(BF16)
            source, target = target, source
        initial = weights[matrix].astype(F32)
        stepped = initial - source[...].astype(F32)
        old_norm = jnp.sqrt(jnp.sum(initial * initial, axis=0, keepdims=True) + epsilon)
        new_norm = jnp.sqrt(jnp.sum(stepped * stepped, axis=0, keepdims=True) + epsilon)
        renewed[matrix] = (stepped * (old_norm / new_norm)).astype(BF16)

    def pass_on(matrix, piece):
        @pl.when(jnp.logical_not(starts(matrix)))
        def _():
            cast_copy(matrix, piece).start()

        side_copy(matrix, piece).start()

    def sum_piece(matrix, piece, behind):
        here = part(piece)
        core_copy(matrix, piece).wait_recv()
        total[matrix, here] += core_in[matrix, here].astype(F32)

        @pl.when(jnp.logical_not(starts(matrix)))
        def _():
            chain_copy(matrix, piece).wait_recv()
            total[matrix, here] += chain_in[matrix, here].astype(F32)

        @pl.when(jnp.logical_not(ends(matrix)))
        def _():
            chain_out[matrix, here] = total[matrix, here].astype(BF16)

            @pl.when(behind)
            def _():
                chain_copy(0, piece).wait_send()

            chain_copy(matrix, piece).start()

    def sum_and_renew(turn, carry):
        matrix = jnp.where(core == 0, 2 * turn, 1)

        @pl.when((core == 0) | (turn == 0))
        def _():
            for piece in range(PIECES):
                sum_piece(matrix, piece, turn == 1)

            @pl.when(ends(matrix))
            def _():
                renew(matrix)
                for piece in range(PIECES):
                    pass_on(matrix, piece)
        return carry

    lax.fori_loop(0, 2, sum_and_renew, 0)

    def take(matrix, piece):
        @pl.when((core == matrix % 2) & jnp.logical_not(ends(matrix)))
        def _():
            cast_copy(matrix, piece).wait_recv()
            pass_on(matrix, piece)

        @pl.when(core != matrix % 2)
        def _():
            side_copy(matrix, piece).wait_recv()

    @pl.when(core == 0)
    def _():
        for matrix in (0, 1):
            for piece in range(PIECES):
                take(matrix, piece)

    @pl.when(core == 1)
    def _():
        for matrix in (1, 0):
            for piece in range(PIECES):
                take(matrix, piece)

    def hide(turn, carry):
        query_rows = queries[flip(head, turn, heads)]
        pre_gate = mat(query_rows, renewed[0])
        pre_up = mat(query_rows, renewed[1])
        hiddens[turn] = (pre_gate * sigmoid(pre_gate) * pre_up).astype(BF16)
        return carry

    def hide_turn(turn, carry):
        query_copy(turn).wait_recv()
        return hide(turn, carry)

    def answer_half(part_index):
        def answer_turn(turn, carry):
            cols = half_columns(part_index)
            answers[turn, :, cols] = mat(hiddens[turn], renewed[2, :, cols]).astype(BF16)
            answer_copy(turn, part_index).start()
            return carry

        lax.fori_loop(1, heads, answer_turn, 0)

    hands_on = (core == 0) & jnp.logical_not(starts(2) | ends(2))

    @pl.when(hands_on)
    def _():
        turn = 1
        for piece in range(PIECES):
            take(2, piece)
            if piece % 2 == 1 and turn < heads:
                hide_turn(turn, 0)
                turn += 1
        lax.fori_loop(turn, heads, hide_turn, 0)
        answer_half(0)
        answer_half(1)

    @pl.when(jnp.logical_not(hands_on))
    def _():
        lax.fori_loop(1, heads, hide_turn, 0)
        for piece in range(PIECES):
            take(2, piece)
            if 2 * (piece + 1) % PIECES == 0:
                answer_half(2 * (piece + 1) // PIECES - 1)

    local[6].wait()
    hide(0, 0)
    answers[0] = mat(hiddens[0], renewed[2]).astype(BF16)

    if attn:
        @pl.when(halo_comes)
        def _():
            halo_copy(0, False).wait_recv()
            halo_copy(1, False).wait_recv()
        attend(0)

    def finish(value, index):
        if attn:
            value = (value.astype(F32) + attended[:, columns(index)]).astype(BF16)
        out[:, columns(index)] = value

    finish(answers[0], head)
    for turn in range(1, heads):
        for part_index in range(2):
            answer_copy(turn, part_index).wait_recv()
        other = flip(head, turn, heads)
        finish(returned[other], other)

    for turn in range(1, heads):
        key_copy(turn).wait_send()
        og_copy(turn).wait_send()
        query_copy(turn).wait_send()
        for part_index in range(2):
            answer_copy(turn, part_index).wait_send()
    if attn:
        @pl.when(halo_sends)
        def _():
            halo_copy(0, False).wait_send()
            halo_copy(1, False).wait_send()

        @pl.when(relay_sends)
        def _():
            relay_copy(0).wait_send()
            relay_copy(1).wait_send()
    for matrix in range(3):
        @pl.when(core != matrix % 2)
        def _():
            for piece in range(PIECES):
                core_copy(matrix, piece).wait_send()

        @pl.when(core == matrix % 2)
        def _():
            for piece in range(PIECES):
                side_copy(matrix, piece).wait_send()

            if matrix > 0:
                @pl.when(jnp.logical_not(ends(matrix)))
                def _():
                    for piece in range(PIECES):
                        chain_copy(matrix, piece).wait_send()

            @pl.when(jnp.logical_not(starts(matrix)))
            def _():
                for piece in range(PIECES):
                    cast_copy(matrix, piece).wait_send()


def memory_call(attn, *arrays):
    arrays = arrays[:3] + (arrays[3].T,) + arrays[4:]
    rows = arrays[0].shape[0]
    heads, width = arrays[4].shape[:2]
    ctx = lax.axis_size("ctx")
    chain = ctx // (2 * heads)
    model = arrays[0].shape[1]
    swa_model = arrays[-1].shape[1]
    square = (width, width)
    tokens = (heads, rows, width)
    dma = pltpu.SemaphoreType.DMA
    scratch = [pltpu.VMEM(tokens, BF16)] * 7
    scratch += [
        pltpu.VMEM((rows, model), BF16),
        pltpu.VMEM((heads, rows), F32),
        pltpu.VMEM((3,) + square, BF16),
        pltpu.VMEM((3,) + square, BF16),
        pltpu.VMEM((3,) + square, F32),
    ]
    scratch += [pltpu.VMEM((3,) + square, BF16)] * 4
    scratch += [pltpu.VMEM(square, BF16)] * 4
    scratch += [dma((10,))]
    scratch += [dma((heads,))] * 6
    scratch += [dma((heads, 2))] * 2
    scratch += [dma((3, PIECES))] * 8
    if attn:
        scratch += [
            pltpu.VMEM((rows, swa_model), BF16),
            pltpu.VMEM((rows + WINDOW, swa_model), BF16),
            pltpu.VMEM((rows + WINDOW, swa_model), BF16),
            pltpu.VMEM((rows, swa_model), F32),
            pltpu.VMEM((2, WINDOW, swa_model), BF16),
        ]
        scratch += [dma((2,))] * 4
    sizes = (ctx, heads, chain, rows, width, swa_model, attn)
    flops = 2 * rows * heads * width * width * 9 + 6 * NS_ITERS * width**3
    return pl.pallas_call(
        functools.partial(kernel, sizes),
        out_shape=jax.ShapeDtypeStruct((rows, model), BF16),
        in_specs=[pl.BlockSpec(memory_space=pl.ANY)] * len(arrays),
        out_specs=pl.BlockSpec(memory_space=pltpu.VMEM),
        scratch_shapes=scratch,
        cost_estimate=pl.CostEstimate(
            flops=flops, bytes_accessed=8 * rows * model * 2, transcendentals=rows * model
        ),
        compiler_params=pltpu.CompilerParams(
            collective_id=0, has_side_effects=True, vmem_limit_bytes=52 * 1024 * 1024
        ),
    )(*arrays)


def passed_along(value, axis, steps):
    count = lax.axis_size(axis)
    first, last = (max(0, -steps), min(count, count - steps))
    return lax.ppermute(value, axis, [(source, source + steps) for source in range(first, last)])


def attend(query_rows, key_window, value_window, device_index):
    row_count = query_rows.shape[0]
    key_count = key_window.shape[0]
    head_total = query_rows.shape[1] // SWA_DH
    query_heads = query_rows.reshape(row_count, head_total, SWA_DH)
    key_heads = key_window.reshape(key_count, head_total, SWA_DH)
    value_heads = value_window.reshape(key_count, head_total, SWA_DH)
    score_scale = 1.0 / math.sqrt(SWA_DH)
    scores = (
        jnp.einsum("qhd,khd->hqk", query_heads, key_heads, preferred_element_type=jnp.float32)
        * score_scale
    )
    query_pos = device_index * row_count + jnp.arange(row_count, dtype=jnp.int32)
    key_pos = device_index * row_count - WINDOW + jnp.arange(key_count, dtype=jnp.int32)
    allowed = (
        (key_pos[None, :] <= query_pos[:, None])
        & (key_pos[None, :] > query_pos[:, None] - WINDOW)
        & (key_pos[None, :] >= 0)
    )
    masked = jnp.where(allowed[None, :, :], scores, -jnp.inf)
    row_peak = jnp.max(masked, axis=-1, keepdims=True)
    exponent = jnp.exp(masked - row_peak)
    row_total = jnp.sum(exponent, axis=-1, keepdims=True)
    weights_bf = (exponent / row_total).astype(jnp.bfloat16)
    result = jnp.einsum("hqk,khd->qhd", weights_bf, value_heads, preferred_element_type=jnp.float32)
    return result.reshape(row_count, head_total * SWA_DH)


def shards(fw_q, fw_k, fw_v, fw_lr, fast_gate, fast_up, fast_down, attn_q, attn_k, attn_v):
    fast = (fw_q, fw_k, fw_v, fw_lr, fast_gate, fast_up, fast_down)
    groups = lax.axis_size("head")
    if groups == 1:
        return memory_call(True, *fast, attn_q, attn_k, attn_v)
    tokens_here = fw_k.shape[0]
    row_count = tokens_here // groups
    device_index = lax.axis_index("ctx") * groups + lax.axis_index("head")
    tail_pairs = passed_along(jnp.stack([attn_k[-WINDOW:], attn_v[-WINDOW:]]), "ctx", 1)
    extended = jnp.concatenate([tail_pairs, jnp.stack([attn_k, attn_v])], axis=1)
    windows = jnp.stack(
        [
            extended[:, group_index * row_count : group_index * row_count + WINDOW + row_count]
            for group_index in range(groups)
        ]
    )
    query_parts = attn_q.reshape(groups, 1, row_count, attn_q.shape[1])
    got_q, got_kv = (
        lax.all_to_all(query_parts, "head", split_axis=0, concat_axis=3, tiled=True),
        lax.all_to_all(windows, "head", split_axis=0, concat_axis=3, tiled=True),
    )
    memory = memory_call(False, *fast)
    memory_rows = lax.all_to_all(memory, "head", split_axis=0, concat_axis=1, tiled=True)
    attended = attend(got_q[0, 0], got_kv[0, 0], got_kv[0, 1], device_index)
    return (memory_rows.astype(jnp.float32) + attended).astype(jnp.bfloat16)


def solution(mesh):
    in_specs = (
        P("ctx", "head"),
        P("ctx", "head"),
        P("ctx", "head"),
        P("ctx", "head"),
        P("head", None, None),
        P("head", None, None),
        P("head", None, None),
        P("ctx", "head"),
        P("ctx", "head"),
        P("ctx", "head"),
    )
    out_specs = P(("ctx", "head"), None)
    return jax.shard_map(shards, mesh=mesh, in_specs=in_specs, out_specs=out_specs, check_vma=False)
```

```python
import functools
import math

import jax
import jax.numpy as jnp
from jax import lax
from jax.experimental import pallas as pl
from jax.experimental.pallas import tpu as pltpu
from jax.sharding import PartitionSpec as P

SWA_DH = 128
WINDOW = 128
NS_ITERS = 2
PIECES = 8

linear_coef = 3.4445
square_coef = -4.775
quartic_coef = 2.0315
epsilon = 1e-06

BF16 = jnp.bfloat16
F32 = jnp.float32
MESH = pl.DeviceIdType.MESH


def mat(left, right):
    return jnp.dot(left, right, preferred_element_type=F32)


def mat_tb(left, right):
    return lax.dot_general(left, right, (((1,), (1,)), ((), ())), preferred_element_type=F32)


def mat_ta(left, right):
    return lax.dot_general(left, right, (((0,), (0,)), ((), ())), preferred_element_type=F32)


def sigmoid(value):
    return 1.0 / (1.0 + jnp.exp(-value))


def flip(index, turn, count):
    bit = 1
    while bit < count:
        turn_bit = lax.rem(lax.div(turn, bit), 2)
        index_bit = lax.rem(lax.div(index, bit), 2)
        index = index + turn_bit * (bit - 2 * bit * index_bit)
        bit *= 2
    return index


def kernel(sizes, *refs):
    ctx, heads, chain, rows, width, model, attn = sizes
    fw_q, fw_k, fw_v, fw_lr, w_gate, w_up, w_down = refs[:7]
    refs = refs[7:]
    if attn:
        attn_q, attn_k, attn_v = refs[:3]
        refs = refs[3:]
    out = refs[0]
    (keys, grads, queries, grad_out, answers, returned, hiddens, gates, ups, values, rates, weights, renewed,
     total, core_out, core_in, chain_out, chain_in, iter_a, iter_b, gram, poly,
     local_sem, key_s, key_r, og_s, og_r, q_s, q_r, ans_s, ans_r,
     core_s, core_r, chain_s, chain_r, cast_s, cast_r, side_s, side_r) = refs[1:40]
    if attn:
        q_rows, key_window, value_window, attended, relay, halo_s, halo_r, relay_s, relay_r = refs[40:]

    me = lax.axis_index("ctx")
    core = lax.rem(me, 2)
    head = lax.rem(lax.div(me, 2), heads)
    z = lax.div(me, 2 * heads)
    mate = me + 1 - 2 * core
    step = 2 * heads
    piece_rows = width // PIECES
    first = lax.rem(me, step) == 0
    last = lax.rem(me, step) == step - 1
    halo_to = me + 1 - jnp.where(last, step, 0)
    halo_from = me - 1 + jnp.where(first, step, 0)
    halo_sends = jnp.logical_not(last) | (z > 0)
    halo_comes = jnp.logical_not(first) | (z > 0)
    relay_sends = last & (z < chain - 1)
    relay_comes = last & (z > 0)

    def partner(turn):
        return me + 2 * (flip(head, turn, heads) - head)

    def columns(index):
        return pl.ds(pl.multiple_of(index * width, 128), width)

    def remote(src, dst, send, recv, device):
        return pltpu.make_async_remote_copy(
            src_ref=src, dst_ref=dst, send_sem=send, recv_sem=recv,
            device_id={"ctx": device}, device_id_type=MESH,
        )

    local = [
        pltpu.make_async_copy(fw_v, values, local_sem.at[0]),
        pltpu.make_async_copy(fw_lr, rates, local_sem.at[1]),
        pltpu.make_async_copy(fw_k.at[:, columns(head)], keys.at[head], local_sem.at[2]),
        pltpu.make_async_copy(w_gate.at[head], weights.at[0], local_sem.at[3]),
        pltpu.make_async_copy(w_up.at[head], weights.at[1], local_sem.at[4]),
        pltpu.make_async_copy(w_down.at[head], weights.at[2], local_sem.at[5]),
        pltpu.make_async_copy(fw_q.at[:, columns(head)], queries.at[head], local_sem.at[6]),
    ]
    if attn:
        local += [
            pltpu.make_async_copy(attn_q, q_rows, local_sem.at[7]),
            pltpu.make_async_copy(attn_k, key_window.at[pl.ds(WINDOW, rows)], local_sem.at[8]),
            pltpu.make_async_copy(attn_v, value_window.at[pl.ds(WINDOW, rows)], local_sem.at[9]),
        ]
    for copy in local:
        copy.start()

    barrier = pltpu.get_barrier_semaphore()

    def greet(device):
        pl.semaphore_signal(barrier, inc=1, device_id={"ctx": device}, device_id_type=MESH)

    for turn in range(1, heads):
        greet(partner(turn))
    greet(mate)
    expected = jnp.int32(heads)
    checks = [(z > 0, me - step), (z < chain - 1, me + step)]
    if attn:
        checks += [(halo_comes, halo_from), (halo_sends, halo_to)]
    for there, device in checks:
        pl.when(there)(functools.partial(greet, device))
        expected = expected + there.astype(jnp.int32)
    pl.semaphore_wait(barrier, expected)

    def key_copy(turn):
        other = flip(head, turn, heads)
        return remote(fw_k.at[:, columns(other)], keys.at[head], key_s.at[turn], key_r.at[turn],
                      partner(turn))

    def og_copy(turn):
        other = flip(head, turn, heads)
        return remote(grad_out.at[other], grads.at[head], og_s.at[turn], og_r.at[turn],
                      partner(turn))

    def query_copy(turn):
        other = flip(head, turn, heads)
        return remote(fw_q.at[:, columns(other)], queries.at[head], q_s.at[turn], q_r.at[turn],
                      partner(turn))

    def half_columns(part_index):
        return pl.ds(part_index * (width // 2), width // 2)

    def answer_copy(turn, part_index):
        cols = half_columns(part_index)
        return remote(answers.at[turn, :, cols], returned.at[head, :, cols],
                      ans_s.at[turn, part_index], ans_r.at[turn, part_index], partner(turn))

    for turn in range(1, heads):
        key_copy(turn).start()
    if attn:
        def relay_copy(which):
            source = (attn_k, attn_v)[which]
            return remote(source.at[pl.ds(rows - WINDOW, WINDOW)], relay.at[which],
                          relay_s.at[which], relay_r.at[which], me + step)

        @pl.when(relay_sends)
        def _():
            relay_copy(0).start()
            relay_copy(1).start()

    local[0].wait()
    local[1].wait()
    rate_columns = jnp.transpose(rates[...])
    for index in range(heads):
        cols = slice(index * width, (index + 1) * width)
        grad_out[index] = (
            -(rate_columns[:, index : index + 1] * values[:, cols].astype(F32))
        ).astype(BF16)
    for turn in range(1, heads - 1):
        og_copy(turn).start()

    def pre_products(turn, key_ref):
        key_rows = key_ref[...]
        gates[turn] = mat(key_rows, weights[0])
        ups[turn] = mat(key_rows, weights[1])

    def accumulate(turn, key_ref, og_ref, first, done=None):
        key_rows = key_ref[...]
        og = og_ref[...]
        pre_gate = gates[turn]
        pre_up = ups[turn]
        hidden_grad = mat_tb(og, weights[2])
        sig = sigmoid(pre_gate)
        activated = pre_gate * sig
        gate_grad = (hidden_grad * pre_up * (sig * (1.0 + pre_gate * (1.0 - sig)))).astype(BF16)
        up_grad = (hidden_grad * activated).astype(BF16)
        hidden = (activated * pre_up).astype(BF16)
        for index, (left, right) in enumerate(
            ((key_rows, gate_grad), (key_rows, up_grad), (hidden, og))
        ):
            if first:
                total[index] = mat_ta(left, right)
            else:
                total[index] += mat_ta(left, right)
            if done is not None:
                done(index)

    for index in range(2, 6):
        local[index].wait()
    pre_products(0, keys.at[head])
    accumulate(0, keys.at[head], grad_out.at[head], True)

    if attn:
        score_scale = 1.0 / math.sqrt(SWA_DH)
        swa_heads = model // SWA_DH
        row_id = lax.broadcasted_iota(jnp.int32, (WINDOW, 2 * WINDOW), 0)
        col_id = lax.broadcasted_iota(jnp.int32, (WINDOW, 2 * WINDOW), 1)

        def attend(block):
            allowed = (col_id > row_id) & (col_id <= row_id + WINDOW)
            if block == 0:
                allowed = allowed & (col_id >= jnp.where(me == 0, WINDOW, 0))
            here = slice(block * WINDOW, (block + 1) * WINDOW)
            there = slice(block * WINDOW, (block + 2) * WINDOW)

            def one(index, carry):
                cols = pl.ds(pl.multiple_of(index * SWA_DH, SWA_DH), SWA_DH)
                scores = mat_tb(q_rows[here, cols], key_window[there, cols]) * score_scale
                masked = jnp.where(allowed, scores, -jnp.inf)
                peak = jnp.max(masked, axis=-1, keepdims=True)
                exponent = jnp.exp(masked - peak)
                probs = (exponent / jnp.sum(exponent, axis=-1, keepdims=True)).astype(BF16)
                attended[here, cols] = mat(probs, value_window[there, cols])
                return carry

            lax.fori_loop(0, swa_heads, one, 0, unroll=4 if swa_heads % 4 == 0 else 1)

        for index in range(7, 10):
            local[index].wait()
        for block in range(1, rows // WINDOW):
            attend(block)

    def root(matrix):
        return jnp.where(matrix == 1, chain - 1, 0)

    def toward(matrix):
        return jnp.where(matrix == 1, 1, -1)

    def part(piece):
        return pl.ds(piece * piece_rows, piece_rows)

    def core_copy(matrix, piece):
        return remote(core_out.at[matrix, part(piece)], core_in.at[matrix, part(piece)],
                      core_s.at[matrix, piece], core_r.at[matrix, piece], mate)

    def chain_copy(matrix, piece):
        return remote(chain_out.at[matrix, part(piece)], chain_in.at[matrix, part(piece)],
                      chain_s.at[matrix, piece], chain_r.at[matrix, piece],
                      me + step * toward(matrix))

    def block(matrix, piece):
        half = width // 2
        cols = 2 * width // PIECES
        return renewed.at[matrix, pl.ds(piece % 2 * half, half), pl.ds(piece // 2 * cols, cols)]

    def cast_copy(matrix, piece):
        here = block(matrix, piece)
        return remote(here, here, cast_s.at[matrix, piece], cast_r.at[matrix, piece],
                      me - step * toward(matrix))

    def side_copy(matrix, piece):
        here = block(matrix, piece)
        return remote(here, here, side_s.at[matrix, piece], side_r.at[matrix, piece], mate)

    def starts(matrix):
        return z == chain - 1 - root(matrix)

    def ends(matrix):
        return z == root(matrix)

    def exchange(matrix):
        @pl.when(core != matrix % 2)
        def _():
            for piece in range(PIECES):
                core_out[matrix, part(piece)] = total[matrix, part(piece)].astype(BF16)
                core_copy(matrix, piece).start()

    def key_turn(turn, carry):
        key_copy(turn).wait_recv()

        @pl.when(turn == heads - 1)
        def _():
            og_copy(turn).start()

        pre_products(turn, keys.at[flip(head, turn, heads)])
        return carry

    def gather_turn(turn, carry, done=None):
        og_copy(turn).wait_recv()
        other = flip(head, turn, heads)
        accumulate(turn, keys.at[other], grads.at[other], False, done)
        return carry

    if heads > 1:
        lax.fori_loop(1, heads, key_turn, 0)
        lax.fori_loop(1, heads - 1, gather_turn, 0)
        gather_turn(heads - 1, 0, exchange)
    else:
        for matrix in range(3):
            exchange(matrix)

    for turn in range(1, heads):
        query_copy(turn).start()

    if attn:
        def halo_copy(which, relayed):
            source = (attn_k, attn_v)[which].at[pl.ds(rows - WINDOW, WINDOW)]
            if relayed:
                source = relay.at[which]
            target = (key_window, value_window)[which]
            return remote(source, target.at[pl.ds(0, WINDOW)],
                          halo_s.at[which], halo_r.at[which], halo_to)

        @pl.when(jnp.logical_not(last))
        def _():
            halo_copy(0, False).start()
            halo_copy(1, False).start()

        @pl.when(relay_comes)
        def _():
            for which in range(2):
                relay_copy(which).wait_recv()
                halo_copy(which, True).start()

        @pl.when(me == 0)
        def _():
            key_window[0:WINDOW] = jnp.zeros((WINDOW, model), BF16)
            value_window[0:WINDOW] = jnp.zeros((WINDOW, model), BF16)

    def renew(matrix):
        gradient = total[matrix]
        norm = jnp.sqrt(jnp.sum(gradient * gradient) + epsilon)
        iter_a[...] = (gradient * (1.0 / norm)).astype(BF16)
        source, target = iter_a, iter_b
        for _ in range(NS_ITERS):
            gram[...] = mat_tb(source[...], source[...]).astype(BF16)
            square = mat(gram[...], gram[...])
            poly[...] = (square_coef * gram[...].astype(F32) + quartic_coef * square).astype(BF16)
            target[...] = (
                linear_coef * source[...].astype(F32) + mat(poly[...], source[...])
            ).astype(BF16)
            source, target = target, source
        initial = weights[matrix].astype(F32)
        stepped = initial - source[...].astype(F32)
        old_norm = jnp.sqrt(jnp.sum(initial * initial, axis=0, keepdims=True) + epsilon)
        new_norm = jnp.sqrt(jnp.sum(stepped * stepped, axis=0, keepdims=True) + epsilon)
        renewed[matrix] = (stepped * (old_norm / new_norm)).astype(BF16)

    def pass_on(matrix, piece):
        @pl.when(jnp.logical_not(starts(matrix)))
        def _():
            cast_copy(matrix, piece).start()

        side_copy(matrix, piece).start()

    def sum_piece(matrix, piece, behind):
        here = part(piece)
        core_copy(matrix, piece).wait_recv()
        total[matrix, here] += core_in[matrix, here].astype(F32)

        @pl.when(jnp.logical_not(starts(matrix)))
        def _():
            chain_copy(matrix, piece).wait_recv()
            total[matrix, here] += chain_in[matrix, here].astype(F32)

        @pl.when(jnp.logical_not(ends(matrix)))
        def _():
            chain_out[matrix, here] = total[matrix, here].astype(BF16)

            @pl.when(behind)
            def _():
                chain_copy(0, piece).wait_send()

            chain_copy(matrix, piece).start()

    def sum_and_renew(turn, carry):
        matrix = jnp.where(core == 0, 2 * turn, 1)

        @pl.when((core == 0) | (turn == 0))
        def _():
            for piece in range(PIECES):
                sum_piece(matrix, piece, turn == 1)

            @pl.when(ends(matrix))
            def _():
                renew(matrix)
                for piece in range(PIECES):
                    pass_on(matrix, piece)
        return carry

    lax.fori_loop(0, 2, sum_and_renew, 0)

    def take(matrix, piece):
        @pl.when((core == matrix % 2) & jnp.logical_not(ends(matrix)))
        def _():
            cast_copy(matrix, piece).wait_recv()
            pass_on(matrix, piece)

        @pl.when(core != matrix % 2)
        def _():
            side_copy(matrix, piece).wait_recv()

    @pl.when(core == 0)
    def _():
        for matrix in (0, 1):
            for piece in range(PIECES):
                take(matrix, piece)

    @pl.when(core == 1)
    def _():
        for matrix in (1, 0):
            for piece in range(PIECES):
                take(matrix, piece)

    def hide(turn, carry):
        query_rows = queries[flip(head, turn, heads)]
        pre_gate = mat(query_rows, renewed[0])
        pre_up = mat(query_rows, renewed[1])
        hiddens[turn] = (pre_gate * sigmoid(pre_gate) * pre_up).astype(BF16)
        return carry

    def hide_turn(turn, carry):
        query_copy(turn).wait_recv()
        return hide(turn, carry)

    def answer_half(part_index):
        def answer_turn(turn, carry):
            cols = half_columns(part_index)
            answers[turn, :, cols] = mat(hiddens[turn], renewed[2, :, cols]).astype(BF16)
            answer_copy(turn, part_index).start()
            return carry

        lax.fori_loop(1, heads, answer_turn, 0)

    hands_on = (core == 0) & jnp.logical_not(starts(2) | ends(2))

    @pl.when(hands_on)
    def _():
        turn = 1
        for piece in range(PIECES):
            take(2, piece)
            if piece % 2 == 1 and turn < heads:
                hide_turn(turn, 0)
                turn += 1
        lax.fori_loop(turn, heads, hide_turn, 0)
        answer_half(0)
        answer_half(1)

    @pl.when(jnp.logical_not(hands_on))
    def _():
        lax.fori_loop(1, heads, hide_turn, 0)
        for piece in range(PIECES):
            take(2, piece)
            if 2 * (piece + 1) % PIECES == 0:
                answer_half(2 * (piece + 1) // PIECES - 1)

    local[6].wait()
    hide(0, 0)
    answers[0] = mat(hiddens[0], renewed[2]).astype(BF16)

    if attn:
        @pl.when(halo_comes)
        def _():
            halo_copy(0, False).wait_recv()
            halo_copy(1, False).wait_recv()
        attend(0)

    def finish(value, index):
        if attn:
            value = (value.astype(F32) + attended[:, columns(index)]).astype(BF16)
        out[:, columns(index)] = value

    finish(answers[0], head)
    for turn in range(1, heads):
        for part_index in range(2):
            answer_copy(turn, part_index).wait_recv()
        other = flip(head, turn, heads)
        finish(returned[other], other)

    for turn in range(1, heads):
        key_copy(turn).wait_send()
        og_copy(turn).wait_send()
        query_copy(turn).wait_send()
        for part_index in range(2):
            answer_copy(turn, part_index).wait_send()
    if attn:
        @pl.when(halo_sends)
        def _():
            halo_copy(0, False).wait_send()
            halo_copy(1, False).wait_send()

        @pl.when(relay_sends)
        def _():
            relay_copy(0).wait_send()
            relay_copy(1).wait_send()
    for matrix in range(3):
        @pl.when(core != matrix % 2)
        def _():
            for piece in range(PIECES):
                core_copy(matrix, piece).wait_send()

        @pl.when(core == matrix % 2)
        def _():
            for piece in range(PIECES):
                side_copy(matrix, piece).wait_send()

            if matrix > 0:
                @pl.when(jnp.logical_not(ends(matrix)))
                def _():
                    for piece in range(PIECES):
                        chain_copy(matrix, piece).wait_send()

            @pl.when(jnp.logical_not(starts(matrix)))
            def _():
                for piece in range(PIECES):
                    cast_copy(matrix, piece).wait_send()


def memory_call(attn, *arrays):
    arrays = arrays[:3] + (arrays[3].T,) + arrays[4:]
    rows = arrays[0].shape[0]
    heads, width = arrays[4].shape[:2]
    ctx = lax.axis_size("ctx")
    chain = ctx // (2 * heads)
    model = arrays[0].shape[1]
    swa_model = arrays[-1].shape[1]
    square = (width, width)
    tokens = (heads, rows, width)
    dma = pltpu.SemaphoreType.DMA
    scratch = [pltpu.VMEM(tokens, BF16)] * 7 + [pltpu.VMEM(tokens, F32)] * 2
    scratch += [
        pltpu.VMEM((rows, model), BF16),
        pltpu.VMEM((heads, rows), F32),
        pltpu.VMEM((3,) + square, BF16),
        pltpu.VMEM((3,) + square, BF16),
        pltpu.VMEM((3,) + square, F32),
    ]
    scratch += [pltpu.VMEM((3,) + square, BF16)] * 4
    scratch += [pltpu.VMEM(square, BF16)] * 4
    scratch += [dma((10,))]
    scratch += [dma((heads,))] * 6
    scratch += [dma((heads, 2))] * 2
    scratch += [dma((3, PIECES))] * 8
    if attn:
        scratch += [
            pltpu.VMEM((rows, swa_model), BF16),
            pltpu.VMEM((rows + WINDOW, swa_model), BF16),
            pltpu.VMEM((rows + WINDOW, swa_model), BF16),
            pltpu.VMEM((rows, swa_model), F32),
            pltpu.VMEM((2, WINDOW, swa_model), BF16),
        ]
        scratch += [dma((2,))] * 4
    sizes = (ctx, heads, chain, rows, width, swa_model, attn)
    flops = 2 * rows * heads * width * width * 9 + 6 * NS_ITERS * width**3
    return pl.pallas_call(
        functools.partial(kernel, sizes),
        out_shape=jax.ShapeDtypeStruct((rows, model), BF16),
        in_specs=[pl.BlockSpec(memory_space=pl.ANY)] * len(arrays),
        out_specs=pl.BlockSpec(memory_space=pltpu.VMEM),
        scratch_shapes=scratch,
        cost_estimate=pl.CostEstimate(
            flops=flops, bytes_accessed=8 * rows * model * 2, transcendentals=rows * model
        ),
        compiler_params=pltpu.CompilerParams(
            collective_id=0, has_side_effects=True, vmem_limit_bytes=52 * 1024 * 1024
        ),
    )(*arrays)


def passed_along(value, axis, steps):
    count = lax.axis_size(axis)
    first, last = (max(0, -steps), min(count, count - steps))
    return lax.ppermute(value, axis, [(source, source + steps) for source in range(first, last)])


def attend(query_rows, key_window, value_window, device_index):
    row_count = query_rows.shape[0]
    key_count = key_window.shape[0]
    head_total = query_rows.shape[1] // SWA_DH
    query_heads = query_rows.reshape(row_count, head_total, SWA_DH)
    key_heads = key_window.reshape(key_count, head_total, SWA_DH)
    value_heads = value_window.reshape(key_count, head_total, SWA_DH)
    score_scale = 1.0 / math.sqrt(SWA_DH)
    scores = (
        jnp.einsum("qhd,khd->hqk", query_heads, key_heads, preferred_element_type=jnp.float32)
        * score_scale
    )
    query_pos = device_index * row_count + jnp.arange(row_count, dtype=jnp.int32)
    key_pos = device_index * row_count - WINDOW + jnp.arange(key_count, dtype=jnp.int32)
    allowed = (
        (key_pos[None, :] <= query_pos[:, None])
        & (key_pos[None, :] > query_pos[:, None] - WINDOW)
        & (key_pos[None, :] >= 0)
    )
    masked = jnp.where(allowed[None, :, :], scores, -jnp.inf)
    row_peak = jnp.max(masked, axis=-1, keepdims=True)
    exponent = jnp.exp(masked - row_peak)
    row_total = jnp.sum(exponent, axis=-1, keepdims=True)
    weights_bf = (exponent / row_total).astype(jnp.bfloat16)
    result = jnp.einsum("hqk,khd->qhd", weights_bf, value_heads, preferred_element_type=jnp.float32)
    return result.reshape(row_count, head_total * SWA_DH)


def shards(fw_q, fw_k, fw_v, fw_lr, fast_gate, fast_up, fast_down, attn_q, attn_k, attn_v):
    fast = (fw_q, fw_k, fw_v, fw_lr, fast_gate, fast_up, fast_down)
    groups = lax.axis_size("head")
    if groups == 1:
        return memory_call(True, *fast, attn_q, attn_k, attn_v)
    tokens_here = fw_k.shape[0]
    row_count = tokens_here // groups
    device_index = lax.axis_index("ctx") * groups + lax.axis_index("head")
    tail_pairs = passed_along(jnp.stack([attn_k[-WINDOW:], attn_v[-WINDOW:]]), "ctx", 1)
    extended = jnp.concatenate([tail_pairs, jnp.stack([attn_k, attn_v])], axis=1)
    windows = jnp.stack(
        [
            extended[:, group_index * row_count : group_index * row_count + WINDOW + row_count]
            for group_index in range(groups)
        ]
    )
    query_parts = attn_q.reshape(groups, 1, row_count, attn_q.shape[1])
    got_q, got_kv = (
        lax.all_to_all(query_parts, "head", split_axis=0, concat_axis=3, tiled=True),
        lax.all_to_all(windows, "head", split_axis=0, concat_axis=3, tiled=True),
    )
    memory = memory_call(False, *fast)
    memory_rows = lax.all_to_all(memory, "head", split_axis=0, concat_axis=1, tiled=True)
    attended = attend(got_q[0, 0], got_kv[0, 0], got_kv[0, 1], device_index)
    return (memory_rows.astype(jnp.float32) + attended).astype(jnp.bfloat16)


def solution(mesh):
    in_specs = (
        P("ctx", "head"),
        P("ctx", "head"),
        P("ctx", "head"),
        P("ctx", "head"),
        P("head", None, None),
        P("head", None, None),
        P("head", None, None),
        P("ctx", "head"),
        P("ctx", "head"),
        P("ctx", "head"),
    )
    out_specs = P(("ctx", "head"), None)
    return jax.shard_map(shards, mesh=mesh, in_specs=in_specs, out_specs=out_specs, check_vma=False)
```

```python
import functools
import math

import jax
import jax.numpy as jnp
from jax import lax
from jax.experimental import pallas as pl
from jax.experimental.pallas import tpu as pltpu
from jax.sharding import PartitionSpec as P

SWA_DH = 128
WINDOW = 128
NS_ITERS = 2
PIECES = 8

linear_coef = 3.4445
square_coef = -4.775
quartic_coef = 2.0315
epsilon = 1e-06

BF16 = jnp.bfloat16
F32 = jnp.float32
MESH = pl.DeviceIdType.MESH


def mat(left, right):
    return jnp.dot(left, right, preferred_element_type=F32)


def mat_tb(left, right):
    return lax.dot_general(left, right, (((1,), (1,)), ((), ())), preferred_element_type=F32)


def mat_ta(left, right):
    return lax.dot_general(left, right, (((0,), (0,)), ((), ())), preferred_element_type=F32)


def sigmoid(value):
    return 1.0 / (1.0 + jnp.exp(-value))


def flip(index, turn, count):
    bit = 1
    while bit < count:
        turn_bit = lax.rem(lax.div(turn, bit), 2)
        index_bit = lax.rem(lax.div(index, bit), 2)
        index = index + turn_bit * (bit - 2 * bit * index_bit)
        bit *= 2
    return index


def kernel(sizes, *refs):
    ctx, heads, chain, rows, width, model, attn = sizes
    fw_q, fw_k, fw_v, fw_lr, w_gate, w_up, w_down = refs[:7]
    refs = refs[7:]
    if attn:
        attn_q, attn_k, attn_v = refs[:3]
        refs = refs[3:]
    out = refs[0]
    (keys, grads, queries, grad_out, answers, returned, hiddens, gates, ups, values, rates, weights, renewed,
     total, core_out, core_in, chain_out, chain_in, iter_a, iter_b, gram, poly,
     local_sem, key_s, key_r, og_s, og_r, q_s, q_r, ans_s, ans_r,
     core_s, core_r, chain_s, chain_r, cast_s, cast_r, side_s, side_r) = refs[1:40]
    if attn:
        q_rows, key_window, value_window, attended, relay, halo_s, halo_r, relay_s, relay_r = refs[40:]

    me = lax.axis_index("ctx")
    core = lax.rem(me, 2)
    head = lax.rem(lax.div(me, 2), heads)
    z = lax.div(me, 2 * heads)
    mate = me + 1 - 2 * core
    step = 2 * heads
    piece_rows = width // PIECES
    first = lax.rem(me, step) == 0
    last = lax.rem(me, step) == step - 1
    halo_to = me + 1 - jnp.where(last, step, 0)
    halo_from = me - 1 + jnp.where(first, step, 0)
    halo_sends = jnp.logical_not(last) | (z > 0)
    halo_comes = jnp.logical_not(first) | (z > 0)
    relay_sends = last & (z < chain - 1)
    relay_comes = last & (z > 0)

    def partner(turn):
        return me + 2 * (flip(head, turn, heads) - head)

    def columns(index):
        return pl.ds(pl.multiple_of(index * width, 128), width)

    def remote(src, dst, send, recv, device):
        return pltpu.make_async_remote_copy(
            src_ref=src, dst_ref=dst, send_sem=send, recv_sem=recv,
            device_id={"ctx": device}, device_id_type=MESH,
        )

    local = [
        pltpu.make_async_copy(fw_v, values, local_sem.at[0]),
        pltpu.make_async_copy(fw_lr, rates, local_sem.at[1]),
        pltpu.make_async_copy(fw_k.at[:, columns(head)], keys.at[head], local_sem.at[2]),
        pltpu.make_async_copy(w_gate.at[head], weights.at[0], local_sem.at[3]),
        pltpu.make_async_copy(w_up.at[head], weights.at[1], local_sem.at[4]),
        pltpu.make_async_copy(w_down.at[head], weights.at[2], local_sem.at[5]),
        pltpu.make_async_copy(fw_q.at[:, columns(head)], queries.at[head], local_sem.at[6]),
    ]
    if attn:
        local += [
            pltpu.make_async_copy(attn_q, q_rows, local_sem.at[7]),
            pltpu.make_async_copy(attn_k, key_window.at[pl.ds(WINDOW, rows)], local_sem.at[8]),
            pltpu.make_async_copy(attn_v, value_window.at[pl.ds(WINDOW, rows)], local_sem.at[9]),
        ]
    for copy in local:
        copy.start()

    barrier = pltpu.get_barrier_semaphore()

    def greet(device):
        pl.semaphore_signal(barrier, inc=1, device_id={"ctx": device}, device_id_type=MESH)

    for turn in range(1, heads):
        greet(partner(turn))
    greet(mate)
    expected = jnp.int32(heads)
    checks = [(z > 0, me - step), (z < chain - 1, me + step)]
    if attn:
        checks += [(halo_comes, halo_from), (halo_sends, halo_to)]
    for there, device in checks:
        pl.when(there)(functools.partial(greet, device))
        expected = expected + there.astype(jnp.int32)
    pl.semaphore_wait(barrier, expected)

    def key_copy(turn):
        other = flip(head, turn, heads)
        return remote(fw_k.at[:, columns(other)], keys.at[head], key_s.at[turn], key_r.at[turn],
                      partner(turn))

    def og_copy(turn):
        other = flip(head, turn, heads)
        return remote(grad_out.at[other], grads.at[head], og_s.at[turn], og_r.at[turn],
                      partner(turn))

    def query_copy(turn):
        other = flip(head, turn, heads)
        return remote(fw_q.at[:, columns(other)], queries.at[head], q_s.at[turn], q_r.at[turn],
                      partner(turn))

    def half_columns(part_index):
        return pl.ds(part_index * (width // 2), width // 2)

    def answer_copy(turn, part_index):
        cols = half_columns(part_index)
        return remote(answers.at[turn, :, cols], returned.at[head, :, cols],
                      ans_s.at[turn, part_index], ans_r.at[turn, part_index], partner(turn))

    for turn in range(1, heads):
        key_copy(turn).start()
    if attn:
        def relay_copy(which):
            source = (attn_k, attn_v)[which]
            return remote(source.at[pl.ds(rows - WINDOW, WINDOW)], relay.at[which],
                          relay_s.at[which], relay_r.at[which], me + step)

        @pl.when(relay_sends)
        def _():
            relay_copy(0).start()
            relay_copy(1).start()

    local[0].wait()
    local[1].wait()
    rate_columns = jnp.transpose(rates[...])
    for index in range(heads):
        cols = slice(index * width, (index + 1) * width)
        grad_out[index] = (
            -(rate_columns[:, index : index + 1] * values[:, cols].astype(F32))
        ).astype(BF16)
    for turn in range(1, heads - 1):
        og_copy(turn).start()

    def pre_products(turn, key_ref):
        key_rows = key_ref[...]
        gates[turn] = mat(key_rows, weights[0])
        ups[turn] = mat(key_rows, weights[1])

    def accumulate(turn, key_ref, og_ref, first, done=None):
        key_rows = key_ref[...]
        og = og_ref[...]
        pre_gate = gates[turn]
        pre_up = ups[turn]
        hidden_grad = mat_tb(og, weights[2])
        sig = sigmoid(pre_gate)
        activated = pre_gate * sig
        gate_grad = (hidden_grad * pre_up * (sig * (1.0 + pre_gate * (1.0 - sig)))).astype(BF16)
        up_grad = (hidden_grad * activated).astype(BF16)
        hidden = (activated * pre_up).astype(BF16)
        for index, (left, right) in enumerate(
            ((key_rows, gate_grad), (key_rows, up_grad), (hidden, og))
        ):
            if first:
                total[index] = mat_ta(left, right)
            else:
                total[index] += mat_ta(left, right)
            if done is not None:
                done(index)

    for index in range(2, 6):
        local[index].wait()
    pre_products(0, keys.at[head])
    accumulate(0, keys.at[head], grad_out.at[head], True)

    if attn:
        score_scale = 1.0 / math.sqrt(SWA_DH)
        swa_heads = model // SWA_DH
        row_id = lax.broadcasted_iota(jnp.int32, (WINDOW, 2 * WINDOW), 0)
        col_id = lax.broadcasted_iota(jnp.int32, (WINDOW, 2 * WINDOW), 1)

        def attend(block):
            allowed = (col_id > row_id) & (col_id <= row_id + WINDOW)
            if block == 0:
                allowed = allowed & (col_id >= jnp.where(me == 0, WINDOW, 0))
            here = slice(block * WINDOW, (block + 1) * WINDOW)
            there = slice(block * WINDOW, (block + 2) * WINDOW)

            def one(index, carry):
                cols = pl.ds(pl.multiple_of(index * SWA_DH, SWA_DH), SWA_DH)
                scores = mat_tb(q_rows[here, cols], key_window[there, cols]) * score_scale
                masked = jnp.where(allowed, scores, -jnp.inf)
                peak = jnp.max(masked, axis=-1, keepdims=True)
                exponent = jnp.exp(masked - peak)
                probs = (exponent * (1.0 / jnp.sum(exponent, axis=-1, keepdims=True))).astype(BF16)
                attended[here, cols] = mat(probs, value_window[there, cols])
                return carry

            lax.fori_loop(0, swa_heads, one, 0, unroll=4 if swa_heads % 4 == 0 else 1)

        for index in range(7, 10):
            local[index].wait()
        for block in range(1, rows // WINDOW):
            attend(block)

    def root(matrix):
        return jnp.where(matrix == 1, chain - 1, 0)

    def toward(matrix):
        return jnp.where(matrix == 1, 1, -1)

    def part(piece):
        return pl.ds(piece * piece_rows, piece_rows)

    def core_copy(matrix, piece):
        return remote(core_out.at[matrix, part(piece)], core_in.at[matrix, part(piece)],
                      core_s.at[matrix, piece], core_r.at[matrix, piece], mate)

    def chain_copy(matrix, piece):
        return remote(chain_out.at[matrix, part(piece)], chain_in.at[matrix, part(piece)],
                      chain_s.at[matrix, piece], chain_r.at[matrix, piece],
                      me + step * toward(matrix))

    def block(matrix, piece):
        half = width // 2
        cols = 2 * width // PIECES
        return renewed.at[matrix, pl.ds(piece % 2 * half, half), pl.ds(piece // 2 * cols, cols)]

    def cast_copy(matrix, piece):
        here = block(matrix, piece)
        return remote(here, here, cast_s.at[matrix, piece], cast_r.at[matrix, piece],
                      me - step * toward(matrix))

    def side_copy(matrix, piece):
        here = block(matrix, piece)
        return remote(here, here, side_s.at[matrix, piece], side_r.at[matrix, piece], mate)

    def starts(matrix):
        return z == chain - 1 - root(matrix)

    def ends(matrix):
        return z == root(matrix)

    def exchange(matrix):
        @pl.when(core != matrix % 2)
        def _():
            for piece in range(PIECES):
                core_out[matrix, part(piece)] = total[matrix, part(piece)].astype(BF16)
                core_copy(matrix, piece).start()

    def key_turn(turn, carry):
        key_copy(turn).wait_recv()

        @pl.when(turn == heads - 1)
        def _():
            og_copy(turn).start()

        pre_products(turn, keys.at[flip(head, turn, heads)])
        return carry

    def gather_turn(turn, carry, done=None):
        og_copy(turn).wait_recv()
        other = flip(head, turn, heads)
        accumulate(turn, keys.at[other], grads.at[other], False, done)
        return carry

    if heads > 1:
        lax.fori_loop(1, heads, key_turn, 0)
        lax.fori_loop(1, heads - 1, gather_turn, 0)
        gather_turn(heads - 1, 0, exchange)
    else:
        for matrix in range(3):
            exchange(matrix)

    for turn in range(1, heads):
        query_copy(turn).start()

    if attn:
        def halo_copy(which, relayed):
            source = (attn_k, attn_v)[which].at[pl.ds(rows - WINDOW, WINDOW)]
            if relayed:
                source = relay.at[which]
            target = (key_window, value_window)[which]
            return remote(source, target.at[pl.ds(0, WINDOW)],
                          halo_s.at[which], halo_r.at[which], halo_to)

        @pl.when(jnp.logical_not(last))
        def _():
            halo_copy(0, False).start()
            halo_copy(1, False).start()

        @pl.when(relay_comes)
        def _():
            for which in range(2):
                relay_copy(which).wait_recv()
                halo_copy(which, True).start()

        @pl.when(me == 0)
        def _():
            key_window[0:WINDOW] = jnp.zeros((WINDOW, model), BF16)
            value_window[0:WINDOW] = jnp.zeros((WINDOW, model), BF16)

    def renew(matrix):
        gradient = total[matrix]
        norm = jnp.sqrt(jnp.sum(gradient * gradient) + epsilon)
        iter_a[...] = (gradient * (1.0 / norm)).astype(BF16)
        source, target = iter_a, iter_b
        for _ in range(NS_ITERS):
            gram[...] = mat_tb(source[...], source[...]).astype(BF16)
            square = mat(gram[...], gram[...])
            poly[...] = (square_coef * gram[...].astype(F32) + quartic_coef * square).astype(BF16)
            target[...] = (
                linear_coef * source[...].astype(F32) + mat(poly[...], source[...])
            ).astype(BF16)
            source, target = target, source
        initial = weights[matrix].astype(F32)
        stepped = initial - source[...].astype(F32)
        old_norm = jnp.sqrt(jnp.sum(initial * initial, axis=0, keepdims=True) + epsilon)
        new_norm = jnp.sqrt(jnp.sum(stepped * stepped, axis=0, keepdims=True) + epsilon)
        renewed[matrix] = (stepped * (old_norm / new_norm)).astype(BF16)

    def pass_on(matrix, piece):
        @pl.when(jnp.logical_not(starts(matrix)))
        def _():
            cast_copy(matrix, piece).start()

        side_copy(matrix, piece).start()

    def sum_piece(matrix, piece, behind):
        here = part(piece)
        core_copy(matrix, piece).wait_recv()
        total[matrix, here] += core_in[matrix, here].astype(F32)

        @pl.when(jnp.logical_not(starts(matrix)))
        def _():
            chain_copy(matrix, piece).wait_recv()
            total[matrix, here] += chain_in[matrix, here].astype(F32)

        @pl.when(jnp.logical_not(ends(matrix)))
        def _():
            chain_out[matrix, here] = total[matrix, here].astype(BF16)

            @pl.when(behind)
            def _():
                chain_copy(0, piece).wait_send()

            chain_copy(matrix, piece).start()

    def sum_and_renew(turn, carry):
        matrix = jnp.where(core == 0, 2 * turn, 1)

        @pl.when((core == 0) | (turn == 0))
        def _():
            for piece in range(PIECES):
                sum_piece(matrix, piece, turn == 1)

            @pl.when(ends(matrix))
            def _():
                renew(matrix)
                for piece in range(PIECES):
                    pass_on(matrix, piece)
        return carry

    lax.fori_loop(0, 2, sum_and_renew, 0)

    def take(matrix, piece):
        @pl.when((core == matrix % 2) & jnp.logical_not(ends(matrix)))
        def _():
            cast_copy(matrix, piece).wait_recv()
            pass_on(matrix, piece)

        @pl.when(core != matrix % 2)
        def _():
            side_copy(matrix, piece).wait_recv()

    @pl.when(core == 0)
    def _():
        for matrix in (0, 1):
            for piece in range(PIECES):
                take(matrix, piece)

    @pl.when(core == 1)
    def _():
        for matrix in (1, 0):
            for piece in range(PIECES):
                take(matrix, piece)

    def hide(turn, carry):
        query_rows = queries[flip(head, turn, heads)]
        pre_gate = mat(query_rows, renewed[0])
        pre_up = mat(query_rows, renewed[1])
        hiddens[turn] = (pre_gate * sigmoid(pre_gate) * pre_up).astype(BF16)
        return carry

    def hide_turn(turn, carry):
        query_copy(turn).wait_recv()
        return hide(turn, carry)

    def answer_half(part_index):
        def answer_turn(turn, carry):
            cols = half_columns(part_index)
            answers[turn, :, cols] = mat(hiddens[turn], renewed[2, :, cols]).astype(BF16)
            answer_copy(turn, part_index).start()
            return carry

        lax.fori_loop(1, heads, answer_turn, 0)

    hands_on = (core == 0) & jnp.logical_not(starts(2) | ends(2))

    @pl.when(hands_on)
    def _():
        turn = 1
        for piece in range(PIECES):
            take(2, piece)
            if piece % 2 == 1 and turn < heads:
                hide_turn(turn, 0)
                turn += 1
        lax.fori_loop(turn, heads, hide_turn, 0)
        answer_half(0)
        answer_half(1)

    @pl.when(jnp.logical_not(hands_on))
    def _():
        lax.fori_loop(1, heads, hide_turn, 0)
        for piece in range(PIECES):
            take(2, piece)
            if 2 * (piece + 1) % PIECES == 0:
                answer_half(2 * (piece + 1) // PIECES - 1)

    local[6].wait()
    hide(0, 0)
    answers[0] = mat(hiddens[0], renewed[2]).astype(BF16)

    if attn:
        @pl.when(halo_comes)
        def _():
            halo_copy(0, False).wait_recv()
            halo_copy(1, False).wait_recv()
        attend(0)

    def finish(value, index):
        if attn:
            value = (value.astype(F32) + attended[:, columns(index)]).astype(BF16)
        out[:, columns(index)] = value

    finish(answers[0], head)
    for turn in range(1, heads):
        for part_index in range(2):
            answer_copy(turn, part_index).wait_recv()
        other = flip(head, turn, heads)
        finish(returned[other], other)

    for turn in range(1, heads):
        key_copy(turn).wait_send()
        og_copy(turn).wait_send()
        query_copy(turn).wait_send()
        for part_index in range(2):
            answer_copy(turn, part_index).wait_send()
    if attn:
        @pl.when(halo_sends)
        def _():
            halo_copy(0, False).wait_send()
            halo_copy(1, False).wait_send()

        @pl.when(relay_sends)
        def _():
            relay_copy(0).wait_send()
            relay_copy(1).wait_send()
    for matrix in range(3):
        @pl.when(core != matrix % 2)
        def _():
            for piece in range(PIECES):
                core_copy(matrix, piece).wait_send()

        @pl.when(core == matrix % 2)
        def _():
            for piece in range(PIECES):
                side_copy(matrix, piece).wait_send()

            if matrix > 0:
                @pl.when(jnp.logical_not(ends(matrix)))
                def _():
                    for piece in range(PIECES):
                        chain_copy(matrix, piece).wait_send()

            @pl.when(jnp.logical_not(starts(matrix)))
            def _():
                for piece in range(PIECES):
                    cast_copy(matrix, piece).wait_send()


def memory_call(attn, *arrays):
    arrays = arrays[:3] + (arrays[3].T,) + arrays[4:]
    rows = arrays[0].shape[0]
    heads, width = arrays[4].shape[:2]
    ctx = lax.axis_size("ctx")
    chain = ctx // (2 * heads)
    model = arrays[0].shape[1]
    swa_model = arrays[-1].shape[1]
    square = (width, width)
    tokens = (heads, rows, width)
    dma = pltpu.SemaphoreType.DMA
    scratch = [pltpu.VMEM(tokens, BF16)] * 7 + [pltpu.VMEM(tokens, F32)] * 2
    scratch += [
        pltpu.VMEM((rows, model), BF16),
        pltpu.VMEM((heads, rows), F32),
        pltpu.VMEM((3,) + square, BF16),
        pltpu.VMEM((3,) + square, BF16),
        pltpu.VMEM((3,) + square, F32),
    ]
    scratch += [pltpu.VMEM((3,) + square, BF16)] * 4
    scratch += [pltpu.VMEM(square, BF16)] * 4
    scratch += [dma((10,))]
    scratch += [dma((heads,))] * 6
    scratch += [dma((heads, 2))] * 2
    scratch += [dma((3, PIECES))] * 8
    if attn:
        scratch += [
            pltpu.VMEM((rows, swa_model), BF16),
            pltpu.VMEM((rows + WINDOW, swa_model), BF16),
            pltpu.VMEM((rows + WINDOW, swa_model), BF16),
            pltpu.VMEM((rows, swa_model), F32),
            pltpu.VMEM((2, WINDOW, swa_model), BF16),
        ]
        scratch += [dma((2,))] * 4
    sizes = (ctx, heads, chain, rows, width, swa_model, attn)
    flops = 2 * rows * heads * width * width * 9 + 6 * NS_ITERS * width**3
    return pl.pallas_call(
        functools.partial(kernel, sizes),
        out_shape=jax.ShapeDtypeStruct((rows, model), BF16),
        in_specs=[pl.BlockSpec(memory_space=pl.ANY)] * len(arrays),
        out_specs=pl.BlockSpec(memory_space=pltpu.VMEM),
        scratch_shapes=scratch,
        cost_estimate=pl.CostEstimate(
            flops=flops, bytes_accessed=8 * rows * model * 2, transcendentals=rows * model
        ),
        compiler_params=pltpu.CompilerParams(
            collective_id=0, has_side_effects=True, vmem_limit_bytes=52 * 1024 * 1024
        ),
    )(*arrays)


def passed_along(value, axis, steps):
    count = lax.axis_size(axis)
    first, last = (max(0, -steps), min(count, count - steps))
    return lax.ppermute(value, axis, [(source, source + steps) for source in range(first, last)])


def attend(query_rows, key_window, value_window, device_index):
    row_count = query_rows.shape[0]
    key_count = key_window.shape[0]
    head_total = query_rows.shape[1] // SWA_DH
    query_heads = query_rows.reshape(row_count, head_total, SWA_DH)
    key_heads = key_window.reshape(key_count, head_total, SWA_DH)
    value_heads = value_window.reshape(key_count, head_total, SWA_DH)
    score_scale = 1.0 / math.sqrt(SWA_DH)
    scores = (
        jnp.einsum("qhd,khd->hqk", query_heads, key_heads, preferred_element_type=jnp.float32)
        * score_scale
    )
    query_pos = device_index * row_count + jnp.arange(row_count, dtype=jnp.int32)
    key_pos = device_index * row_count - WINDOW + jnp.arange(key_count, dtype=jnp.int32)
    allowed = (
        (key_pos[None, :] <= query_pos[:, None])
        & (key_pos[None, :] > query_pos[:, None] - WINDOW)
        & (key_pos[None, :] >= 0)
    )
    masked = jnp.where(allowed[None, :, :], scores, -jnp.inf)
    row_peak = jnp.max(masked, axis=-1, keepdims=True)
    exponent = jnp.exp(masked - row_peak)
    row_total = jnp.sum(exponent, axis=-1, keepdims=True)
    weights_bf = (exponent / row_total).astype(jnp.bfloat16)
    result = jnp.einsum("hqk,khd->qhd", weights_bf, value_heads, preferred_element_type=jnp.float32)
    return result.reshape(row_count, head_total * SWA_DH)


def shards(fw_q, fw_k, fw_v, fw_lr, fast_gate, fast_up, fast_down, attn_q, attn_k, attn_v):
    fast = (fw_q, fw_k, fw_v, fw_lr, fast_gate, fast_up, fast_down)
    groups = lax.axis_size("head")
    if groups == 1:
        return memory_call(True, *fast, attn_q, attn_k, attn_v)
    tokens_here = fw_k.shape[0]
    row_count = tokens_here // groups
    device_index = lax.axis_index("ctx") * groups + lax.axis_index("head")
    tail_pairs = passed_along(jnp.stack([attn_k[-WINDOW:], attn_v[-WINDOW:]]), "ctx", 1)
    extended = jnp.concatenate([tail_pairs, jnp.stack([attn_k, attn_v])], axis=1)
    windows = jnp.stack(
        [
            extended[:, group_index * row_count : group_index * row_count + WINDOW + row_count]
            for group_index in range(groups)
        ]
    )
    query_parts = attn_q.reshape(groups, 1, row_count, attn_q.shape[1])
    got_q, got_kv = (
        lax.all_to_all(query_parts, "head", split_axis=0, concat_axis=3, tiled=True),
        lax.all_to_all(windows, "head", split_axis=0, concat_axis=3, tiled=True),
    )
    memory = memory_call(False, *fast)
    memory_rows = lax.all_to_all(memory, "head", split_axis=0, concat_axis=1, tiled=True)
    attended = attend(got_q[0, 0], got_kv[0, 0], got_kv[0, 1], device_index)
    return (memory_rows.astype(jnp.float32) + attended).astype(jnp.bfloat16)


def solution(mesh):
    in_specs = (
        P("ctx", "head"),
        P("ctx", "head"),
        P("ctx", "head"),
        P("ctx", "head"),
        P("head", None, None),
        P("head", None, None),
        P("head", None, None),
        P("ctx", "head"),
        P("ctx", "head"),
        P("ctx", "head"),
    )
    out_specs = P(("ctx", "head"), None)
    return jax.shard_map(shards, mesh=mesh, in_specs=in_specs, out_specs=out_specs, check_vma=False)
```
